768 devices in a mesh: seq: 24 (over y, z_lo), tensor: 32 (over z_hi, x, core).
Axes of the slice: x: 4, y: 8, z: 12 (z_hi: 4, z_lo: 3; z = z_hi * 3 + z_lo), core: 2. Of those that a mesh axis runs over, the one named last changes fastest.
Arguments:
- frames: bfloat16 [18432, 1536], P('seq'), may hold values from -6 to 6
- w_up: bfloat16 [1536, 6144], P(None, 'tensor'), may hold values from -0.15625 to 0.15625
- w_down: bfloat16 [6144, 1536], P('tensor'), may hold values from -0.078125 to 0.078125
- kernel: float32 [31, 1536], P(None, 'tensor'), may hold values from -1 to 1
- utt_bounds: int32 [2, 18432], P(None, 'seq'), may hold values from 0 to 18432, as said below
- cotangent: bfloat16 [18432, 1536], P('seq', 'tensor'), may hold values from -6 to 6
Outputs:
- output: bfloat16 [18432, 1536], P('seq', 'tensor')
- grad_w_up: float32 [1536, 6144], P(None, 'tensor')
- grad_w_down: float32 [6144, 1536], P('tensor')
- grad_kernel: float32 [31, 1536], P(None, 'tensor')
The draws below stay inside these ranges and needn't reach their ends.
Inputs may be any that keep to these rules, and one draw needn't show every extreme that they name: Utterances are contiguous runs of frames; for every frame t, utt_bounds[0, t] <= t < utt_bounds[1, t], and all frames of one utterance carry the same pair. Utterances hold 48 to min(800, 9216) frames, except the last, which the stream's end may cut.
All inputs are finite; a program needn't handle non-finite values.
Results may differ from the reference program's by a relative error of at most 0.0061.
Values may be sent and summed in bfloat16 or wider, within the bound.
A program may use at most 64 MiB of HBM per device.

```python
import math
import jax
import jax.numpy as jnp
from jax import lax

D = 1536
FF = 6144
K = 31
TOTAL = 18432


def draw_utt_bounds(key, part):
    key = jax.random.fold_in(key, 7)
    count = TOTAL // 48 + 2
    longest = max(48, min(800, TOTAL // 2))
    lengths = jax.random.randint(key, (count,), 48, longest + 1, dtype=jnp.int32)
    edges = jnp.concatenate([jnp.zeros((1,), jnp.int32), jnp.cumsum(lengths).astype(jnp.int32)])
    position = jnp.arange(TOTAL, dtype=jnp.int32)
    which = (jnp.searchsorted(edges, position, side='right') - 1).astype(jnp.int32)
    starts = edges[which]
    ends = jnp.minimum(edges[which + 1], TOTAL)
    return jnp.stack([starts, ends]).astype(jnp.int32)


def steps_of(rng, extent, shards, smallest, largest):
    def one(dim, parts):
        heights = jax.random.uniform(jax.random.fold_in(jax.random.fold_in(rng, 6), dim), (parts,), jnp.float32, smallest / len(shards), largest / len(shards))
        return jnp.repeat(jnp.exp(heights), extent[dim] // parts).reshape((-1,) + (1,) * (len(extent) - dim - 1))

    loudness = one(*shards[0])
    for cut in shards[1:]:
        loudness = loudness * one(*cut)
    return loudness


def noise(rng, shape, scale, limit, shards=(), held_as=jnp.bfloat16):
    level = steps_of(rng, shape, shards, -0.22, 0.18) if shards else 1.0
    drawn = jax.random.normal(rng, shape, jnp.float32) * scale * level
    return jnp.minimum(jnp.maximum(drawn, -limit), limit).astype(held_as)


def setup_inputs(seed: int = 0) -> dict:
    splits = jax.random.split(jax.random.key(seed), 7)
    frames = noise(splits[0], (TOTAL, D), 1.0, 6.0, ((0, 24),))
    w_up = noise(splits[1], (D, FF), D ** -0.5, 0.15625, ((1, 32),))
    w_down = noise(splits[2], (FF, D), FF ** -0.5, 0.078125, ((0, 32),))
    kernel = noise(splits[3], (K, D), K ** -0.5, 1.0, ((1, 32),), jnp.float32)
    utt_bounds = draw_utt_bounds(jax.random.fold_in(splits[6], 71), 0)
    cotangent = noise(splits[5], (TOTAL, D), 1.0, 6.0, ((0, 24), (1, 32)))
    return {"frames": frames, "w_up": w_up, "w_down": w_down, "kernel": kernel, "utt_bounds": utt_bounds, "cotangent": cotangent}


def reference(frames, w_up, w_down, kernel, utt_bounds, cotangent):
    half = K // 2
    wide = frames.astype(jnp.float32)
    mean = lax.optimization_barrier(jnp.mean(wide, axis=1, keepdims=True))
    centred = wide - mean
    var = lax.optimization_barrier(jnp.mean(centred * centred, axis=1, keepdims=True))
    normed = (centred / jnp.sqrt(var + 1e-05)).astype(jnp.bfloat16)
    act = jnp.dot(normed, w_up, preferred_element_type=jnp.float32)
    act_sig = jax.nn.sigmoid(act)
    hidden = (act * act_sig).astype(jnp.bfloat16)
    mixed = (wide + 0.5 * jnp.dot(hidden, w_down, preferred_element_type=jnp.float32)).astype(jnp.bfloat16)
    position = jnp.arange(TOTAL, dtype=jnp.int32)
    masks = []
    for tap in range(K):
        target = position + (tap - half)
        inside = (target >= utt_bounds[0]) & (target < utt_bounds[1])
        masks.append(inside.astype(jnp.float32)[:, None])
    mixed_pad = jnp.pad(mixed.astype(jnp.float32), ((half, half), (0, 0)))
    conv = jnp.zeros((TOTAL, D), jnp.float32)
    for tap in range(K):
        conv = conv + kernel[tap][None, :] * mixed_pad[tap:tap + TOTAL] * masks[tap]
    conv_sig = jax.nn.sigmoid(conv)
    output = (mixed.astype(jnp.float32) + conv * conv_sig).astype(jnp.bfloat16)
    grad_conv = cotangent.astype(jnp.float32) * conv_sig * (1.0 + conv * (1.0 - conv_sig))
    grad_pad = jnp.pad(grad_conv, ((half, half), (0, 0)))
    grad_glu = jnp.zeros((TOTAL, D), jnp.float32)
    kernel_terms = []
    for tap in range(K):
        mirror = 2 * half - tap
        grad_glu = grad_glu + kernel[tap][None, :] * grad_pad[mirror:mirror + TOTAL] * masks[mirror]
        kernel_terms.append(lax.optimization_barrier(jnp.sum(grad_conv * mixed_pad[tap:tap + TOTAL] * masks[tap], axis=0)))
    grad_mixed = (cotangent.astype(jnp.float32) + grad_glu).astype(jnp.bfloat16)
    grad_hidden = 0.5 * jnp.dot(grad_mixed, w_down.T, preferred_element_type=jnp.float32)
    grad_act = (grad_hidden * act_sig * (1.0 + act * (1.0 - act_sig))).astype(jnp.bfloat16)
    scale = 1.0 / math.sqrt(TOTAL)
    grad_w_up = jnp.dot(normed.T, grad_act, preferred_element_type=jnp.float32) * scale
    grad_w_down = 0.5 * jnp.dot(hidden.T, grad_mixed, preferred_element_type=jnp.float32) * scale
    grad_kernel = jnp.stack(kernel_terms) * scale
    return (output, grad_w_up, grad_w_down, grad_kernel)
```

```python
import math

import jax
import jax.numpy as jnp
from jax import lax
from jax.experimental import pallas as pl
from jax.experimental.pallas import tpu as pltpu
from jax.sharding import PartitionSpec as P

MESH = pl.DeviceIdType.MESH
K = 31
HALF = K // 2
NY, NW, NZ, NX = 8, 3, 4, 4
LANES = 128
WAYS = ((1, 3), (3, 1))
HOPS = ((4, 3), (3, 4))
COPIES = 109
F32, BF16 = jnp.float32, jnp.bfloat16


def flip(index, mask):
    if mask == 0:
        return index
    if mask == 1:
        return index + 1 - 2 * lax.rem(index, 2)
    if mask == 2:
        return lax.rem(index + 2, 4)
    return 3 - index


def relative(place, way):
    first, second = WAYS[way]
    return (first if place & 1 else 0) ^ (second if place & 2 else 0)


def dot(a, b, a_dim, b_dim):
    return lax.dot_general(a, b, (((a_dim,), (b_dim,)), ((), ())), preferred_element_type=F32)


def kernel(
    frames,
    w_up,
    w_down,
    taps,
    bounds,
    cot,
    out_t,
    kernel_sum,
    grads,
    normed,
    w_up_t,
    w_down_t,
    ordered,
    act,
    sig,
    hidden,
    keep,
    rs_send,
    rs_recv,
    own,
    x_ext,
    cot_ext,
    edge_send,
    edge_recv,
    cot_send,
    cot_recv,
    masks,
    tap_box,
    gathered,
    piece,
    grad_act,
    totals,
    ring_send,
    ring_recv,
    cross_send,
    cross_recv,
    whole,
    kernel_ring,
    kernel_cross,
    send_sems,
    recv_sems,
):
    length, depth = frames.shape
    width = taps.shape[1]
    hid = w_up.shape[1]
    ext = length + 2 * LANES
    seq, ten = lax.axis_index("seq"), lax.axis_index("tensor")
    y, w = lax.div(seq, NW), lax.rem(seq, NW)
    core, x, z = lax.rem(ten, 2), lax.rem(lax.div(ten, 2), NX), lax.div(ten, 2 * NX)

    def tensor_at(z, x, core):
        return (z * NX + x) * 2 + core

    def x_way(mask):
        return (seq, tensor_at(z, flip(x, mask), core))

    def z_way(mask):
        return (seq, tensor_at(flip(z, mask), x, core))

    def y_way(step):
        return (lax.rem(y + NY + step, NY) * NW + w, ten)

    def w_way(step):
        return (y * NW + lax.rem(w + step, NW), ten)

    sibling = (seq, tensor_at(z, x, 1 - core))
    count = NY * NW
    after = (lax.rem(seq + 1, count), ten)
    before = (lax.rem(seq + count - 1, count), ten)

    barrier = pltpu.get_barrier_semaphore()
    partners = [sibling, x_way(1), x_way(3), z_way(1), z_way(3), after, before]
    partners += [y_way(1), y_way(-1), w_way(1), w_way(2)]
    for partner in partners:
        pl.semaphore_signal(barrier, inc=1, device_id=partner, device_id_type=MESH)

    started = []

    def send(src, dst, target):
        spot = len(started)
        copy = pltpu.make_async_remote_copy(
            src_ref=src,
            dst_ref=dst,
            send_sem=send_sems.at[spot],
            recv_sem=recv_sems.at[spot],
            device_id=target,
            device_id_type=MESH,
        )
        copy.start()
        started.append(copy)
        return copy

    block = LANES

    def normalise(i, carry):
        rows = pl.ds(pl.multiple_of(i * block, block), block)
        wide = frames[rows, :].astype(F32)
        mean = jnp.mean(wide, axis=1, keepdims=True)
        centred = wide - mean
        var = jnp.mean(centred * centred, axis=1, keepdims=True)
        normed[rows, :] = (centred / jnp.sqrt(var + 1e-05)).astype(BF16)
        return carry

    lax.fori_loop(0, length // block, normalise, 0)
    w_up_t[...] = w_up[...].astype(F32).T.astype(BF16)
    w_down_t[...] = w_down[...].astype(F32).T.astype(BF16)
    for way in range(2):
        for c in range(2):
            for i in range(NX):
                for j in range(NZ):
                    home = tensor_at(
                        flip(z, relative(j, way)),
                        flip(x, relative(i, way)),
                        1 - core if c else core,
                    )
                    spot = (c * NX + i) * NZ + j
                    ordered[way, spot * width : (spot + 1) * width, :] = w_down_t[
                        pl.ds(pl.multiple_of(home * width, 16), width), :
                    ]
    up = dot(w_up_t[...], normed[...], 1, 1)
    gate = jax.nn.sigmoid(up)
    act[...] = up
    sig[...] = gate
    hidden[...] = (up * gate).astype(BF16)
    cot_t = dot(
        (
            lax.broadcasted_iota(jnp.int32, (width, width), 0)
            == lax.broadcasted_iota(jnp.int32, (width, width), 1)
        ).astype(BF16),
        cot[...],
        1,
        1,
    )
    cot_ext[:, LANES : LANES + length] = cot_t
    cot_send[0] = cot_t[:, length - LANES :].astype(BF16)
    cot_send[1] = cot_t[:, :LANES].astype(BF16)

    pl.semaphore_wait(barrier, len(partners))

    half = depth // 2
    starts, height = [], half
    offset = 0
    for _ in range(5):
        starts.append((offset, height))
        offset += height
        height //= 2
    chunks = length // LANES
    units = [((i, 0), (chunks - 1 - i, 1)) for i in range(chunks // 2)]

    def rs_start(stage, chunk, way):
        first, second = WAYS[way]
        target = (sibling, x_way(second), x_way(first), z_way(second), z_way(first))[stage]
        low, rows = starts[stage]
        return send(
            rs_send.at[chunk, pl.ds(low, rows), :], rs_recv.at[chunk, pl.ds(low, rows), :], target
        )

    flights = {}
    for unit in units:
        for chunk, way in unit:
            columns = slice(chunk * LANES, (chunk + 1) * LANES)
            part = hidden[:, columns]
            rs_send[chunk, 0:half, :] = dot(ordered[way, half:, :], part, 1, 0).astype(BF16)
            flights[0, chunk] = rs_start(0, chunk, way)
        for chunk, way in unit:
            columns = slice(chunk * LANES, (chunk + 1) * LANES)
            keep[chunk] = dot(ordered[way, :half, :], hidden[:, columns], 1, 0)

    cot_copies = [
        send(cot_send.at[0], cot_recv.at[0], after),
        send(cot_send.at[1], cot_recv.at[1], before),
    ]

    pick = (
        lax.broadcasted_iota(jnp.int32, (width, depth), 1)
        == ten * width + lax.broadcasted_iota(jnp.int32, (width, depth), 0)
    ).astype(BF16)
    own[...] = dot(pick, frames[...], 1, 1)
    limits = bounds[...]
    limits = jnp.concatenate(
        [
            jnp.broadcast_to(limits[:, :1], (2, LANES)),
            limits,
            jnp.broadcast_to(limits[:, length - 1 :], (2, LANES)),
        ],
        axis=1,
    )
    lower = jnp.broadcast_to(limits[0:1, :], (8, ext))
    upper = jnp.broadcast_to(limits[1:2, :], (8, ext))
    spots = seq * length - LANES + lax.broadcasted_iota(jnp.int32, (8, ext), 1)
    for tap in range(K):
        target = spots + (tap - HALF)
        masks[tap] = jnp.where((target >= lower) & (target < upper), 1.0, 0.0).astype(F32)
    tap_box[...] = jnp.zeros((LANES, LANES), F32)
    tap_box[0:K, 0:width] = taps[...]
    tap_box[...] = tap_box[...].T

    edges = {}

    def rs_finish(stage, chunk, way):
        flights[stage, chunk].wait_recv()
        low, rows = starts[stage]
        if stage < 4:
            mid = rows // 2
            nxt = starts[stage + 1][0]
            rs_send[chunk, nxt : nxt + mid, :] = (
                keep[chunk, mid:rows, :] + rs_recv[chunk, low + mid : low + rows, :].astype(F32)
            ).astype(BF16)
            flights[stage + 1, chunk] = rs_start(stage + 1, chunk, way)
            keep[chunk, 0:mid, :] = keep[chunk, 0:mid, :] + rs_recv[
                chunk, low : low + mid, :
            ].astype(F32)
            return
        columns = slice(chunk * LANES, (chunk + 1) * LANES)
        branch = keep[chunk, 0:rows, :] + rs_recv[chunk, low : low + rows, :].astype(F32)
        mixed = (own[:, columns] + 0.5 * branch).astype(BF16)
        x_ext[:, (chunk + 1) * LANES : (chunk + 2) * LANES] = mixed.astype(F32)
        if chunk == 0:
            edge_send[1] = mixed
            edges[1] = send(edge_send.at[1], edge_recv.at[1], before)
        if chunk == chunks - 1:
            edge_send[0] = mixed
            edges[0] = send(edge_send.at[0], edge_recv.at[0], after)

    for turn in range(len(units) + 4):
        for stage in range(5):
            if 0 <= turn - stage < len(units):
                for chunk, way in units[turn - stage]:
                    rs_finish(stage, chunk, way)

    for side, low in ((0, 0), (1, ext - LANES)):
        cot_copies[side].wait_recv()
        cot_ext[:, low : low + LANES] = cot_recv[side].astype(F32)
    for side, low in ((0, 0), (1, ext - LANES)):
        edges[side].wait_recv()
        x_ext[:, low : low + LANES] = edge_recv[side].astype(F32)

    lane = lax.broadcasted_iota(jnp.int32, (8, LANES), 1)
    groups = width // 16
    columns_of = (slice(0, length // 2), slice(length // 2, length))
    inner = slice(LANES, LANES + length)

    def convolve(group):
        rows = pl.ds(pl.multiple_of(group * 8, 8), 8)
        here = x_ext[rows, :]
        cot_here = cot_ext[rows, :]
        tap_here = tap_box[rows, :]
        conv = jnp.zeros((8, ext), F32)
        for tap in range(K):
            moved = pltpu.roll(here, (HALF - tap) % ext, 1) if tap != HALF else here
            conv = conv + tap_here[:, tap : tap + 1] * (moved * masks[tap])
        conv_sig = jax.nn.sigmoid(conv)
        grad = cot_here * conv_sig * (1.0 + conv * (1.0 - conv_sig))
        out_t[rows, :] = (here + conv * conv_sig)[:, inner]
        total = cot_here
        sums = jnp.zeros((8, LANES), F32)
        here = here[:, inner]
        for tap in range(K):
            moved = pltpu.roll(grad, (tap - HALF) % ext, 1) if tap != HALF else grad
            moved = moved * masks[K - 1 - tap]
            total = total + tap_here[:, tap : tap + 1] * moved
            term = jnp.sum(moved[:, inner] * here, axis=1, keepdims=True)
            sums = jnp.where(lane == tap, term, sums)
        kernel_ring[y, rows, :] = sums
        return total[:, inner]

    ag = {}

    def ag_start(stage, unit, way):
        first, second = WAYS[way]
        target = (z_way(first), z_way(second), x_way(first), x_way(second), sibling)[stage]
        rows = 16 << stage
        return send(
            gathered.at[unit, way, pl.ds(0, rows), :],
            gathered.at[unit, way, pl.ds(rows, rows), :],
            target,
        )

    for unit in range(groups):
        grad_mixed = jnp.concatenate([convolve(2 * unit), convolve(2 * unit + 1)], axis=0)
        for way in range(2):
            gathered[unit, way, 0:16, :] = grad_mixed[:, columns_of[way]].astype(BF16)
            ag[0, unit, way] = ag_start(0, unit, way)

    taps_flight = {}

    def taps_start(hop):
        for step, hops in ((1, 4), (-1, 3)):
            if hop > hops:
                continue
            spot = lax.rem(y + NY - step * (hop - 1), NY)
            taps_flight[hop, step] = send(kernel_ring.at[spot], kernel_ring.at[spot], y_way(step))

    def taps_wait(hop):
        for step in (1, -1):
            if (hop, step) in taps_flight:
                taps_flight[hop, step].wait_recv()

    taps_start(1)

    def ag_finish(stage, unit):
        for way in range(2):
            ag[stage, unit, way].wait_recv()
            if stage < 4:
                ag[stage + 1, unit, way] = ag_start(stage + 1, unit, way)
                continue
            for c in range(2):
                for i in range(NX):
                    for j in range(NZ):
                        home = tensor_at(
                            flip(z, relative(j, way)),
                            flip(x, relative(i, way)),
                            1 - core if c else core,
                        )
                        spot = (c * NX + i) * NZ + j
                        piece[
                            pl.ds(pl.multiple_of(home * width + 16 * unit, 16), 16),
                            columns_of[way],
                        ] = gathered[unit, way, spot * 16 : (spot + 1) * 16, :]

    for turn in range(groups + 4):
        for stage in range(5):
            if 0 <= turn - stage < groups:
                ag_finish(stage, turn - stage)
        if turn in (1, 2, 3):
            taps_wait(turn)
            taps_start(turn + 1)
    taps_wait(4)
    total = kernel_ring[0]
    for i in range(1, NY):
        total = total + kernel_ring[i]
    kernel_cross[w] = total
    cross = [send(kernel_cross.at[w], kernel_cross.at[w], w_way(step)) for step in (1, 2)]

    tall, broad = hid // 2, depth // 4

    def down_chunk(d):
        low, left = tall * (d % 2), broad * (d // 2)
        totals[0, d] = dot(hidden[low : low + tall, :], piece[left : left + broad, :], 1, 1)

    def up_chunk(d):
        low, left = tall * (d % 2), broad * (d // 2)
        totals[1, d] = dot(grad_act[low : low + tall, :], normed[:, left : left + broad], 1, 0)

    ring = {}

    def ring_spot(stream, side, k):
        return (stream * 2 + side) * 4 + k - 1

    def ring_start(stream, side, k):
        step = (1, -1)[side]
        if k > HOPS[stream][side]:
            return
        chunk = lax.rem(y + NY + step * k, NY)
        value = totals[stream, chunk]
        if k < HOPS[stream][side]:
            ring[stream, side, k + 1].wait_recv()
            value = value + ring_recv[ring_spot(stream, side, k + 1)].astype(F32)
        spot = ring_spot(stream, side, k)
        ring_send[spot] = value.astype(BF16)
        ring[stream, side, k] = send(ring_send.at[spot], ring_recv.at[spot], y_way(step))

    for d in range(8):
        down_chunk(d)
    ring_start(0, 0, 4)
    ring_start(0, 1, 3)
    grad_hidden = 0.5 * dot(w_down[...], piece[...], 1, 0)
    gate = sig[...]
    grad_act[...] = (grad_hidden * gate * (1.0 + act[...] * (1.0 - gate))).astype(BF16)
    for d in range(8):
        up_chunk(d)
    ring_start(1, 1, 4)
    ring_start(1, 0, 3)
    ring_start(0, 0, 3)
    ring_start(1, 1, 3)
    for k in (2, 1):
        ring_start(0, 1, k)
        ring_start(1, 0, k)
        ring_start(0, 0, k)
        ring_start(1, 1, k)

    third = tall // NW
    cross_flight = {}
    for stream in range(2):
        for side in range(2):
            ring[stream, side, 1].wait_recv()
        totals[stream, y] = (
            totals[stream, y]
            + ring_recv[ring_spot(stream, 0, 1)].astype(F32)
            + ring_recv[ring_spot(stream, 1, 1)].astype(F32)
        )
        for step in (1, 2):
            rows = pl.ds(pl.multiple_of(lax.rem(w + step, NW) * third, third), third)
            cross_send[stream * 2 + step - 1] = totals[stream, y, rows, :].astype(BF16)
            cross_flight[stream, step] = send(
                cross_send.at[stream * 2 + step - 1],
                cross_recv.at[stream * 2 + step - 1],
                w_way(step),
            )
    for copy in cross:
        copy.wait_recv()
    kernel_sum[...] = kernel_cross[0] + kernel_cross[1] + kernel_cross[2]
    mine = pl.ds(pl.multiple_of(w * third, third), third)
    share = {}
    for stream in range(2):
        value = totals[stream, y, mine, :]
        for step in (1, 2):
            cross_flight[stream, step].wait_recv()
            value = value + cross_recv[stream * 2 + step - 1].astype(F32)
        whole[stream, y, mine, :] = value.astype(BF16)
        for step in (1, 2):
            share[stream, step] = send(
                whole.at[stream, y, mine, :], whole.at[stream, y, mine, :], w_way(step)
            )
    spread = {}
    for k in range(1, 6):
        for stream in range(2):
            if k == 1:
                for step in (1, 2):
                    share[stream, step].wait_recv()
            for side in range(2):
                step = (1, -1)[side]
                if 1 < k <= HOPS[stream][side] + 1:
                    spread[stream, side, k - 1].wait_recv()
                if k <= HOPS[stream][side]:
                    spot = lax.rem(y + NY - step * (k - 1), NY)
                    spread[stream, side, k] = send(
                        whole.at[stream, spot], whole.at[stream, spot], y_way(step)
                    )
    grads[...] = whole[...]
    for copy in started:
        copy.wait_send()


def body(frames, w_up, w_down, taps, bounds, cot):
    length, depth = frames.shape
    width = taps.shape[1]
    hid = w_up.shape[1]
    ext = length + 2 * LANES
    chunks = length // LANES
    rs_rows = depth // 2 + depth // 4 + depth // 8 + depth // 16 + depth // 32
    block = (hid // 2, depth // 4)
    vmem = pl.BlockSpec(memory_space=pltpu.VMEM)
    out_t, kernel_sum, grads = pl.pallas_call(
        kernel,
        out_shape=(
            jax.ShapeDtypeStruct((width, length), F32),
            jax.ShapeDtypeStruct((width, LANES), F32),
            jax.ShapeDtypeStruct((2, NY, *block), BF16),
        ),
        in_specs=[vmem] * 6,
        out_specs=(vmem,) * 3,
        scratch_shapes=[
            pltpu.VMEM((length, depth), BF16),
            pltpu.VMEM((hid, depth), BF16),
            pltpu.VMEM((depth, hid), BF16),
            pltpu.VMEM((2, depth, hid), BF16),
            pltpu.VMEM((hid, length), F32),
            pltpu.VMEM((hid, length), F32),
            pltpu.VMEM((hid, length), BF16),
            pltpu.VMEM((chunks, depth // 2, LANES), F32),
            pltpu.VMEM((chunks, rs_rows, LANES), BF16),
            pltpu.VMEM((chunks, rs_rows, LANES), BF16),
            pltpu.VMEM((width, length), F32),
            pltpu.VMEM((width, ext), F32),
            pltpu.VMEM((width, ext), F32),
            pltpu.VMEM((2, width, LANES), BF16),
            pltpu.VMEM((2, width, LANES), BF16),
            pltpu.VMEM((2, width, LANES), BF16),
            pltpu.VMEM((2, width, LANES), BF16),
            pltpu.VMEM((K, 8, ext), F32),
            pltpu.VMEM((LANES, LANES), F32),
            pltpu.VMEM((width // 16, 2, depth // width * 16, length // 2), BF16),
            pltpu.VMEM((depth, length), BF16),
            pltpu.VMEM((hid, length), BF16),
            pltpu.VMEM((2, NY, *block), F32),
            pltpu.VMEM((16, *block), BF16),
            pltpu.VMEM((16, *block), BF16),
            pltpu.VMEM((4, block[0] // NW, block[1]), BF16),
            pltpu.VMEM((4, block[0] // NW, block[1]), BF16),
            pltpu.VMEM((2, NY, *block), BF16),
            pltpu.VMEM((NY, width, LANES), F32),
            pltpu.VMEM((NW, width, LANES), F32),
            pltpu.SemaphoreType.DMA((COPIES,)),
            pltpu.SemaphoreType.DMA((COPIES,)),
        ],
        compiler_params=pltpu.CompilerParams(
            collective_id=0, has_side_effects=True, vmem_limit_bytes=60 << 20
        ),
    )(frames, w_up, w_down, taps, bounds, cot)
    scale = 1.0 / math.sqrt(length * NY * NW)
    down, up = (
        part.reshape(4, 2, *block).transpose(1, 2, 0, 3).reshape(hid, depth).astype(F32)
        for part in (grads[0], grads[1])
    )
    output = out_t.astype(BF16).T
    return output, up.T * scale, down * (0.5 * scale), kernel_sum[:, :K].T * scale


def solution(mesh):
    return jax.shard_map(
        body,
        mesh=mesh,
        in_specs=(
            P("seq", None),
            P(None, "tensor"),
            P("tensor", None),
            P(None, "tensor"),
            P(None, "seq"),
            P("seq", "tensor"),
        ),
        out_specs=(P("seq", "tensor"), P(None, "tensor"), P("tensor", None), P(None, "tensor")),
        check_vma=False,
    )
```

```python
import math

import jax
import jax.numpy as jnp
from jax import lax
from jax.experimental import pallas as pl
from jax.experimental.pallas import tpu as pltpu
from jax.sharding import PartitionSpec as P

MESH = pl.DeviceIdType.MESH
K = 31
HALF = K // 2
NY, NW, NZ, NX = 8, 3, 4, 4
LANES = 128
WAYS = ((1, 3), (3, 1))
HOPS = ((4, 3), (3, 4))
COPIES = 109
F32, BF16 = jnp.float32, jnp.bfloat16


def flip(index, mask):
    if mask == 0:
        return index
    if mask == 1:
        return index + 1 - 2 * lax.rem(index, 2)
    if mask == 2:
        return lax.rem(index + 2, 4)
    return 3 - index


def relative(place, way):
    first, second = WAYS[way]
    return (first if place & 1 else 0) ^ (second if place & 2 else 0)


def dot(a, b, a_dim, b_dim):
    return lax.dot_general(a, b, (((a_dim,), (b_dim,)), ((), ())), preferred_element_type=F32)


def kernel(
    frames,
    w_up_t,
    w_down,
    taps,
    bounds,
    cot_t,
    out_t,
    kernel_sum,
    grads,
    normed,
    w_down_t,
    ordered,
    act,
    sig,
    hidden,
    keep,
    rs_send,
    rs_recv,
    own,
    x_ext,
    cot_ext,
    edge_send,
    edge_recv,
    cot_send,
    cot_recv,
    masks,
    tap_box,
    gathered,
    piece,
    grad_act,
    totals,
    ring_send,
    ring_recv,
    cross_send,
    cross_recv,
    whole,
    kernel_ring,
    kernel_cross,
    send_sems,
    recv_sems,
):
    length, depth = frames.shape
    width = taps.shape[1]
    hid = w_up_t.shape[0]
    ext = length + 2 * LANES
    seq, ten = lax.axis_index("seq"), lax.axis_index("tensor")
    y, w = lax.div(seq, NW), lax.rem(seq, NW)
    core, x, z = lax.rem(ten, 2), lax.rem(lax.div(ten, 2), NX), lax.div(ten, 2 * NX)

    def tensor_at(z, x, core):
        return (z * NX + x) * 2 + core

    def x_way(mask):
        return (seq, tensor_at(z, flip(x, mask), core))

    def z_way(mask):
        return (seq, tensor_at(flip(z, mask), x, core))

    def y_way(step):
        return (lax.rem(y + NY + step, NY) * NW + w, ten)

    def w_way(step):
        return (y * NW + lax.rem(w + step, NW), ten)

    sibling = (seq, tensor_at(z, x, 1 - core))
    count = NY * NW
    after = (lax.rem(seq + 1, count), ten)
    before = (lax.rem(seq + count - 1, count), ten)

    barrier = pltpu.get_barrier_semaphore()
    partners = [sibling, x_way(1), x_way(3), z_way(1), z_way(3), after, before]
    partners += [y_way(1), y_way(-1), w_way(1), w_way(2)]
    for partner in partners:
        pl.semaphore_signal(barrier, inc=1, device_id=partner, device_id_type=MESH)

    started = []

    def send(src, dst, target):
        spot = len(started)
        copy = pltpu.make_async_remote_copy(
            src_ref=src,
            dst_ref=dst,
            send_sem=send_sems.at[spot],
            recv_sem=recv_sems.at[spot],
            device_id=target,
            device_id_type=MESH,
        )
        copy.start()
        started.append(copy)
        return copy

    block = LANES

    def normalise(i, carry):
        rows = pl.ds(pl.multiple_of(i * block, block), block)
        wide = frames[rows, :].astype(F32)
        mean = jnp.mean(wide, axis=1, keepdims=True)
        centred = wide - mean
        var = jnp.mean(centred * centred, axis=1, keepdims=True)
        normed[rows, :] = (centred / jnp.sqrt(var + 1e-05)).astype(BF16)
        return carry

    lax.fori_loop(0, length // block, normalise, 0)
    w_down_t[...] = w_down[...].astype(F32).T.astype(BF16)
    for way in range(2):
        for c in range(2):
            for i in range(NX):
                for j in range(NZ):
                    home = tensor_at(
                        flip(z, relative(j, way)),
                        flip(x, relative(i, way)),
                        1 - core if c else core,
                    )
                    spot = (c * NX + i) * NZ + j
                    ordered[way, spot * width : (spot + 1) * width, :] = w_down_t[
                        pl.ds(pl.multiple_of(home * width, 16), width), :
                    ]
    up = dot(w_up_t[...], normed[...], 1, 1)
    gate = jax.nn.sigmoid(up)
    act[...] = up
    sig[...] = gate
    hidden[...] = (up * gate).astype(BF16)
    cot_ext[:, LANES : LANES + length] = cot_t[...].astype(F32)
    cot_send[0] = cot_t[:, length - LANES :]
    cot_send[1] = cot_t[:, :LANES]

    pl.semaphore_wait(barrier, len(partners))

    half = depth // 2
    starts, height = [], half
    offset = 0
    for _ in range(5):
        starts.append((offset, height))
        offset += height
        height //= 2
    chunks = length // LANES
    units = [((i, 0), (chunks - 1 - i, 1)) for i in range(chunks // 2)]

    def rs_start(stage, chunk, way):
        first, second = WAYS[way]
        target = (sibling, x_way(second), x_way(first), z_way(second), z_way(first))[stage]
        low, rows = starts[stage]
        return send(
            rs_send.at[chunk, pl.ds(low, rows), :], rs_recv.at[chunk, pl.ds(low, rows), :], target
        )

    flights = {}
    for unit in units:
        for chunk, way in unit:
            columns = slice(chunk * LANES, (chunk + 1) * LANES)
            part = hidden[:, columns]
            rs_send[chunk, 0:half, :] = dot(ordered[way, half:, :], part, 1, 0).astype(BF16)
            flights[0, chunk] = rs_start(0, chunk, way)
        for chunk, way in unit:
            columns = slice(chunk * LANES, (chunk + 1) * LANES)
            keep[chunk] = dot(ordered[way, :half, :], hidden[:, columns], 1, 0)

    cot_copies = [
        send(cot_send.at[0], cot_recv.at[0], after),
        send(cot_send.at[1], cot_recv.at[1], before),
    ]

    pick = (
        lax.broadcasted_iota(jnp.int32, (width, depth), 1)
        == ten * width + lax.broadcasted_iota(jnp.int32, (width, depth), 0)
    ).astype(BF16)
    own[...] = dot(pick, frames[...], 1, 1)
    limits = bounds[...]
    limits = jnp.concatenate(
        [
            jnp.broadcast_to(limits[:, :1], (2, LANES)),
            limits,
            jnp.broadcast_to(limits[:, length - 1 :], (2, LANES)),
        ],
        axis=1,
    )
    lower = jnp.broadcast_to(limits[0:1, :], (8, ext))
    upper = jnp.broadcast_to(limits[1:2, :], (8, ext))
    spots = seq * length - LANES + lax.broadcasted_iota(jnp.int32, (8, ext), 1)
    for tap in range(K):
        target = spots + (tap - HALF)
        masks[tap] = jnp.where((target >= lower) & (target < upper), 1.0, 0.0).astype(F32)
    tap_box[...] = jnp.zeros((LANES, LANES), F32)
    tap_box[0:K, 0:width] = taps[...]
    tap_box[...] = tap_box[...].T

    edges = {}

    def rs_finish(stage, chunk, way):
        flights[stage, chunk].wait_recv()
        low, rows = starts[stage]
        if stage < 4:
            mid = rows // 2
            nxt = starts[stage + 1][0]
            rs_send[chunk, nxt : nxt + mid, :] = (
                keep[chunk, mid:rows, :] + rs_recv[chunk, low + mid : low + rows, :].astype(F32)
            ).astype(BF16)
            flights[stage + 1, chunk] = rs_start(stage + 1, chunk, way)
            keep[chunk, 0:mid, :] = keep[chunk, 0:mid, :] + rs_recv[
                chunk, low : low + mid, :
            ].astype(F32)
            return
        columns = slice(chunk * LANES, (chunk + 1) * LANES)
        branch = keep[chunk, 0:rows, :] + rs_recv[chunk, low : low + rows, :].astype(F32)
        mixed = (own[:, columns] + 0.5 * branch).astype(BF16)
        x_ext[:, (chunk + 1) * LANES : (chunk + 2) * LANES] = mixed.astype(F32)
        if chunk == 0:
            edge_send[1] = mixed
            edges[1] = send(edge_send.at[1], edge_recv.at[1], before)
        if chunk == chunks - 1:
            edge_send[0] = mixed
            edges[0] = send(edge_send.at[0], edge_recv.at[0], after)

    for turn in range(len(units) + 4):
        for stage in range(5):
            if 0 <= turn - stage < len(units):
                for chunk, way in units[turn - stage]:
                    rs_finish(stage, chunk, way)

    for side, low in ((0, 0), (1, ext - LANES)):
        cot_copies[side].wait_recv()
        cot_ext[:, low : low + LANES] = cot_recv[side].astype(F32)
    for side, low in ((0, 0), (1, ext - LANES)):
        edges[side].wait_recv()
        x_ext[:, low : low + LANES] = edge_recv[side].astype(F32)

    lane = lax.broadcasted_iota(jnp.int32, (8, LANES), 1)
    groups = width // 16
    columns_of = (slice(0, length // 2), slice(length // 2, length))
    inner = slice(LANES, LANES + length)

    def convolve(group):
        rows = pl.ds(pl.multiple_of(group * 8, 8), 8)
        here = x_ext[rows, :]
        cot_here = cot_ext[rows, :]
        tap_here = tap_box[rows, :]
        conv = jnp.zeros((8, ext), F32)
        for tap in range(K):
            moved = pltpu.roll(here, (HALF - tap) % ext, 1) if tap != HALF else here
            conv = conv + tap_here[:, tap : tap + 1] * (moved * masks[tap])
        conv_sig = jax.nn.sigmoid(conv)
        grad = cot_here * conv_sig * (1.0 + conv * (1.0 - conv_sig))
        output = (here + conv * conv_sig)[:, inner]
        total = cot_here
        sums = jnp.zeros((8, LANES), F32)
        here = here[:, inner]
        for tap in range(K):
            moved = pltpu.roll(grad, (tap - HALF) % ext, 1) if tap != HALF else grad
            moved = moved * masks[K - 1 - tap]
            total = total + tap_here[:, tap : tap + 1] * moved
            term = jnp.sum(moved[:, inner] * here, axis=1, keepdims=True)
            sums = jnp.where(lane == tap, term, sums)
        kernel_ring[y, rows, :] = sums
        return output, total[:, inner]

    ag = {}

    def ag_start(stage, unit, way):
        first, second = WAYS[way]
        target = (z_way(first), z_way(second), x_way(first), x_way(second), sibling)[stage]
        rows = 16 << stage
        return send(
            gathered.at[unit, way, pl.ds(0, rows), :],
            gathered.at[unit, way, pl.ds(rows, rows), :],
            target,
        )

    for unit in range(groups):
        parts = [convolve(2 * unit), convolve(2 * unit + 1)]
        output, grad_mixed = (jnp.concatenate(pair, axis=0) for pair in zip(*parts))
        out_t[16 * unit : 16 * unit + 16, :] = output.astype(BF16)
        for way in range(2):
            gathered[unit, way, 0:16, :] = grad_mixed[:, columns_of[way]].astype(BF16)
            ag[0, unit, way] = ag_start(0, unit, way)

    taps_flight = {}

    def taps_start(hop):
        for step, hops in ((1, 4), (-1, 3)):
            if hop > hops:
                continue
            spot = lax.rem(y + NY - step * (hop - 1), NY)
            taps_flight[hop, step] = send(kernel_ring.at[spot], kernel_ring.at[spot], y_way(step))

    def taps_wait(hop):
        for step in (1, -1):
            if (hop, step) in taps_flight:
                taps_flight[hop, step].wait_recv()

    taps_start(1)

    def ag_finish(stage, unit):
        for way in range(2):
            ag[stage, unit, way].wait_recv()
            if stage < 4:
                ag[stage + 1, unit, way] = ag_start(stage + 1, unit, way)
                continue
            for c in range(2):
                for i in range(NX):
                    for j in range(NZ):
                        home = tensor_at(
                            flip(z, relative(j, way)),
                            flip(x, relative(i, way)),
                            1 - core if c else core,
                        )
                        spot = (c * NX + i) * NZ + j
                        piece[
                            pl.ds(pl.multiple_of(home * width + 16 * unit, 16), 16),
                            columns_of[way],
                        ] = gathered[unit, way, spot * 16 : (spot + 1) * 16, :]

    for turn in range(groups + 4):
        for stage in range(5):
            if 0 <= turn - stage < groups:
                ag_finish(stage, turn - stage)
        if turn in (1, 2, 3):
            taps_wait(turn)
            taps_start(turn + 1)
    taps_wait(4)
    total = kernel_ring[0]
    for i in range(1, NY):
        total = total + kernel_ring[i]
    kernel_cross[w] = total
    cross = [send(kernel_cross.at[w], kernel_cross.at[w], w_way(step)) for step in (1, 2)]

    tall, broad = hid // 2, depth // 4

    def down_chunk(d):
        low, left = tall * (d % 2), broad * (d // 2)
        totals[0, d] = dot(hidden[low : low + tall, :], piece[left : left + broad, :], 1, 1)

    def up_chunk(d):
        low, left = tall * (d % 2), broad * (d // 2)
        totals[1, d] = dot(grad_act[low : low + tall, :], normed[:, left : left + broad], 1, 0)

    ring = {}

    def ring_spot(stream, side, k):
        return (stream * 2 + side) * 4 + k - 1

    def ring_start(stream, side, k):
        step = (1, -1)[side]
        if k > HOPS[stream][side]:
            return
        chunk = lax.rem(y + NY + step * k, NY)
        value = totals[stream, chunk]
        if k < HOPS[stream][side]:
            ring[stream, side, k + 1].wait_recv()
            value = value + ring_recv[ring_spot(stream, side, k + 1)].astype(F32)
        spot = ring_spot(stream, side, k)
        ring_send[spot] = value.astype(BF16)
        ring[stream, side, k] = send(ring_send.at[spot], ring_recv.at[spot], y_way(step))

    for d in range(8):
        down_chunk(d)
    ring_start(0, 0, 4)
    ring_start(0, 1, 3)
    grad_hidden = 0.5 * dot(w_down[...], piece[...], 1, 0)
    gate = sig[...]
    grad_act[...] = (grad_hidden * gate * (1.0 + act[...] * (1.0 - gate))).astype(BF16)
    for d in range(8):
        up_chunk(d)
    ring_start(1, 1, 4)
    ring_start(1, 0, 3)
    ring_start(0, 0, 3)
    ring_start(1, 1, 3)
    for k in (2, 1):
        ring_start(0, 1, k)
        ring_start(1, 0, k)
        ring_start(0, 0, k)
        ring_start(1, 1, k)

    third = tall // NW
    cross_flight = {}
    for stream in range(2):
        for side in range(2):
            ring[stream, side, 1].wait_recv()
        totals[stream, y] = (
            totals[stream, y]
            + ring_recv[ring_spot(stream, 0, 1)].astype(F32)
            + ring_recv[ring_spot(stream, 1, 1)].astype(F32)
        )
        for step in (1, 2):
            rows = pl.ds(pl.multiple_of(lax.rem(w + step, NW) * third, third), third)
            cross_send[stream * 2 + step - 1] = totals[stream, y, rows, :].astype(BF16)
            cross_flight[stream, step] = send(
                cross_send.at[stream * 2 + step - 1],
                cross_recv.at[stream * 2 + step - 1],
                w_way(step),
            )
    for copy in cross:
        copy.wait_recv()
    scale = 1.0 / math.sqrt(length * count)
    tap_box[0:width, :] = (kernel_cross[0] + kernel_cross[1] + kernel_cross[2]) * scale
    kernel_sum[...] = tap_box[...].T[0:K, 0:width]
    mine = pl.ds(pl.multiple_of(w * third, third), third)
    share = {}
    for stream in range(2):
        value = totals[stream, y, mine, :]
        for step in (1, 2):
            cross_flight[stream, step].wait_recv()
            value = value + cross_recv[stream * 2 + step - 1].astype(F32)
        whole[stream, y, mine, :] = value.astype(BF16)
        for step in (1, 2):
            share[stream, step] = send(
                whole.at[stream, y, mine, :], whole.at[stream, y, mine, :], w_way(step)
            )
    spread = {}
    for k in range(1, 6):
        for stream in range(2):
            if k == 1:
                for step in (1, 2):
                    share[stream, step].wait_recv()
            for side in range(2):
                step = (1, -1)[side]
                if 1 < k <= HOPS[stream][side] + 1:
                    spread[stream, side, k - 1].wait_recv()
                if k <= HOPS[stream][side]:
                    spot = lax.rem(y + NY - step * (k - 1), NY)
                    spread[stream, side, k] = send(
                        whole.at[stream, spot], whole.at[stream, spot], y_way(step)
                    )
    for stream in range(2):
        for d in range(8):
            low, left = tall * (d % 2), broad * (d // 2)
            grads[stream, low : low + tall, left : left + broad] = whole[stream, d]
    for copy in started:
        copy.wait_send()


def body(frames, w_up, w_down, taps, bounds, cot):
    length, depth = frames.shape
    width = taps.shape[1]
    hid = w_up.shape[1]
    ext = length + 2 * LANES
    chunks = length // LANES
    rs_rows = depth // 2 + depth // 4 + depth // 8 + depth // 16 + depth // 32
    block = (hid // 2, depth // 4)
    vmem = pl.BlockSpec(memory_space=pltpu.VMEM)
    out_t, kernel_sum, grads = pl.pallas_call(
        kernel,
        out_shape=(
            jax.ShapeDtypeStruct((width, length), BF16),
            jax.ShapeDtypeStruct((K, width), F32),
            jax.ShapeDtypeStruct((2, hid, depth), BF16),
        ),
        in_specs=[vmem] * 6,
        out_specs=(vmem,) * 3,
        scratch_shapes=[
            pltpu.VMEM((length, depth), BF16),
            pltpu.VMEM((depth, hid), BF16),
            pltpu.VMEM((2, depth, hid), BF16),
            pltpu.VMEM((hid, length), F32),
            pltpu.VMEM((hid, length), F32),
            pltpu.VMEM((hid, length), BF16),
            pltpu.VMEM((chunks, depth // 2, LANES), F32),
            pltpu.VMEM((chunks, rs_rows, LANES), BF16),
            pltpu.VMEM((chunks, rs_rows, LANES), BF16),
            pltpu.VMEM((width, length), F32),
            pltpu.VMEM((width, ext), F32),
            pltpu.VMEM((width, ext), F32),
            pltpu.VMEM((2, width, LANES), BF16),
            pltpu.VMEM((2, width, LANES), BF16),
            pltpu.VMEM((2, width, LANES), BF16),
            pltpu.VMEM((2, width, LANES), BF16),
            pltpu.VMEM((K, 8, ext), F32),
            pltpu.VMEM((LANES, LANES), F32),
            pltpu.VMEM((width // 16, 2, depth // width * 16, length // 2), BF16),
            pltpu.VMEM((depth, length), BF16),
            pltpu.VMEM((hid, length), BF16),
            pltpu.VMEM((2, NY, *block), F32),
            pltpu.VMEM((16, *block), BF16),
            pltpu.VMEM((16, *block), BF16),
            pltpu.VMEM((4, block[0] // NW, block[1]), BF16),
            pltpu.VMEM((4, block[0] // NW, block[1]), BF16),
            pltpu.VMEM((2, NY, *block), BF16),
            pltpu.VMEM((NY, width, LANES), F32),
            pltpu.VMEM((NW, width, LANES), F32),
            pltpu.SemaphoreType.DMA((COPIES,)),
            pltpu.SemaphoreType.DMA((COPIES,)),
        ],
        compiler_params=pltpu.CompilerParams(
            collective_id=0, has_side_effects=True, vmem_limit_bytes=60 << 20
        ),
    )(frames, w_up.T, w_down, taps, bounds, cot.T)
    scale = 1.0 / math.sqrt(length * NY * NW)
    down, up = grads[0].astype(F32) * (0.5 * scale), grads[1].astype(F32) * scale
    return out_t.T, up.T, down, kernel_sum


def solution(mesh):
    return jax.shard_map(
        body,
        mesh=mesh,
        in_specs=(
            P("seq", None),
            P(None, "tensor"),
            P("tensor", None),
            P(None, "tensor"),
            P(None, "seq"),
            P("seq", "tensor"),
        ),
        out_specs=(P("seq", "tensor"), P(None, "tensor"), P("tensor", None), P(None, "tensor")),
        check_vma=False,
    )
```

```python
import math

import jax
import jax.numpy as jnp
from jax import lax
from jax.experimental import pallas as pl
from jax.experimental.pallas import tpu as pltpu
from jax.sharding import PartitionSpec as P

MESH = pl.DeviceIdType.MESH
K = 31
HALF = K // 2
NY, NW, NZ, NX = 8, 3, 4, 4
LANES = 128
WAYS = ((1, 3), (3, 1))
HOPS = ((4, 3), (3, 4))
COPIES = 109
F32, BF16 = jnp.float32, jnp.bfloat16


def flip(index, mask):
    if mask == 0:
        return index
    if mask == 1:
        return index + 1 - 2 * lax.rem(index, 2)
    if mask == 2:
        return lax.rem(index + 2, 4)
    return 3 - index


def relative(place, way):
    first, second = WAYS[way]
    return (first if place & 1 else 0) ^ (second if place & 2 else 0)


def dot(a, b, a_dim, b_dim):
    return lax.dot_general(a, b, (((a_dim,), (b_dim,)), ((), ())), preferred_element_type=F32)


def kernel(
    frames,
    w_up_t,
    w_down,
    taps,
    bounds,
    cot_t,
    out_t,
    kernel_sum,
    grads,
    normed,
    w_down_t,
    ordered,
    act,
    sig,
    hidden,
    keep,
    rs_send,
    rs_recv,
    own,
    x_wide,
    cot_wide,
    x_tall,
    cot_tall,
    grad_tall,
    out_tall,
    first_tall,
    last_tall,
    edge_send,
    edge_recv,
    cot_send,
    cot_recv,
    masks,
    tap_box,
    tap_sums,
    gathered,
    piece,
    grad_act,
    totals,
    ring_send,
    ring_recv,
    cross_send,
    cross_recv,
    whole,
    kernel_ring,
    kernel_cross,
    send_sems,
    recv_sems,
):
    length, depth = frames.shape
    width = taps.shape[1]
    hid = w_up_t.shape[0]
    side_length = length // 2
    ext = side_length + 2 * LANES
    seq, ten = lax.axis_index("seq"), lax.axis_index("tensor")
    y, w = lax.div(seq, NW), lax.rem(seq, NW)
    core, x, z = lax.rem(ten, 2), lax.rem(lax.div(ten, 2), NX), lax.div(ten, 2 * NX)

    def tensor_at(z, x, core):
        return (z * NX + x) * 2 + core

    def x_way(mask):
        return (seq, tensor_at(z, flip(x, mask), core))

    def z_way(mask):
        return (seq, tensor_at(flip(z, mask), x, core))

    def y_way(step):
        return (lax.rem(y + NY + step, NY) * NW + w, ten)

    def w_way(step):
        return (y * NW + lax.rem(w + step, NW), ten)

    sibling = (seq, tensor_at(z, x, 1 - core))
    count = NY * NW
    after = (lax.rem(seq + 1, count), ten)
    before = (lax.rem(seq + count - 1, count), ten)

    barrier = pltpu.get_barrier_semaphore()
    partners = [sibling, x_way(1), x_way(3), z_way(1), z_way(3), after, before]
    partners += [y_way(1), y_way(-1), w_way(1), w_way(2)]
    for partner in partners:
        pl.semaphore_signal(barrier, inc=1, device_id=partner, device_id_type=MESH)

    started = []

    def send(src, dst, target):
        spot = len(started)
        copy = pltpu.make_async_remote_copy(
            src_ref=src,
            dst_ref=dst,
            send_sem=send_sems.at[spot],
            recv_sem=recv_sems.at[spot],
            device_id=target,
            device_id_type=MESH,
        )
        copy.start()
        started.append(copy)
        return copy

    block = LANES

    def normalise(i, carry):
        rows = pl.ds(pl.multiple_of(i * block, block), block)
        wide = frames[rows, :].astype(F32)
        mean = jnp.mean(wide, axis=1, keepdims=True)
        centred = wide - mean
        var = jnp.mean(centred * centred, axis=1, keepdims=True)
        normed[rows, :] = (centred / jnp.sqrt(var + 1e-05)).astype(BF16)
        return carry

    lax.fori_loop(0, length // block, normalise, 0)
    w_down_t[...] = w_down[...].astype(F32).T.astype(BF16)
    for way in range(2):
        for c in range(2):
            for i in range(NX):
                for j in range(NZ):
                    home = tensor_at(
                        flip(z, relative(j, way)),
                        flip(x, relative(i, way)),
                        1 - core if c else core,
                    )
                    spot = (c * NX + i) * NZ + j
                    ordered[way, spot * width : (spot + 1) * width, :] = w_down_t[
                        pl.ds(pl.multiple_of(home * width, 16), width), :
                    ]
    up = dot(w_up_t[...], normed[...], 1, 1)
    gate = jax.nn.sigmoid(up)
    act[...] = up
    sig[...] = gate
    hidden[...] = (up * gate).astype(BF16)
    cot_send[0] = cot_t[:, length - LANES :]
    cot_send[1] = cot_t[:, :LANES]

    pl.semaphore_wait(barrier, len(partners))

    half = depth // 2
    starts, height = [], half
    offset = 0
    for _ in range(5):
        starts.append((offset, height))
        offset += height
        height //= 2
    chunks = length // LANES
    units = [((i, 0), (chunks - 1 - i, 1)) for i in range(chunks // 2)]

    def rs_start(stage, chunk, way):
        first, second = WAYS[way]
        target = (sibling, x_way(second), x_way(first), z_way(second), z_way(first))[stage]
        low, rows = starts[stage]
        return send(
            rs_send.at[chunk, pl.ds(low, rows), :], rs_recv.at[chunk, pl.ds(low, rows), :], target
        )

    flights = {}
    for unit in units:
        for chunk, way in unit:
            columns = slice(chunk * LANES, (chunk + 1) * LANES)
            part = hidden[:, columns]
            rs_send[chunk, 0:half, :] = dot(ordered[way, half:, :], part, 1, 0).astype(BF16)
            flights[0, chunk] = rs_start(0, chunk, way)
        for chunk, way in unit:
            columns = slice(chunk * LANES, (chunk + 1) * LANES)
            keep[chunk] = dot(ordered[way, :half, :], hidden[:, columns], 1, 0)

    cot_copies = [
        send(cot_send.at[0], cot_recv.at[0], after),
        send(cot_send.at[1], cot_recv.at[1], before),
    ]

    pick = (
        lax.broadcasted_iota(jnp.int32, (width, depth), 1)
        == ten * width + lax.broadcasted_iota(jnp.int32, (width, depth), 0)
    ).astype(BF16)
    own[...] = dot(pick, frames[...], 1, 1)
    def place(wide, block, value):
        if block <= ext // LANES - 2:
            wide[0:width, (block + 1) * LANES : (block + 2) * LANES] = value
        shifted = block - side_length // LANES
        if shifted >= -1:
            wide[64 : 64 + width, (shifted + 1) * LANES : (shifted + 2) * LANES] = value

    def turn_round(wide, tall):
        for low in range(0, ext, LANES):
            tall[low : low + LANES, :] = wide[:, low : low + LANES].T

    x_wide[...] = jnp.zeros_like(x_wide)
    cot_wide[...] = jnp.zeros_like(cot_wide)
    for block in range(chunks):
        place(cot_wide, block, cot_t[:, block * LANES : (block + 1) * LANES].astype(F32))
    limits = bounds[...]
    limits = jnp.concatenate(
        [
            jnp.broadcast_to(limits[:, :1], (2, LANES)),
            limits,
            jnp.broadcast_to(limits[:, length - 1 :], (2, LANES)),
        ],
        axis=1,
    )
    spots = seq * length - LANES + lax.broadcasted_iota(jnp.int32, limits.shape, 1)
    limits = (limits - spots).astype(F32)
    for row, tall in ((0, first_tall), (1, last_tall)):
        for low in range(0, ext, LANES):
            tall[low : low + LANES, :] = jnp.concatenate(
                [
                    jnp.broadcast_to(limits[row : row + 1, low + i : low + i + LANES], (64, LANES))
                    for i in (0, side_length)
                ],
                axis=0,
            ).T
    first_row, last_row = LANES - 16, LANES + side_length + 16
    for low in range(first_row, last_row, 32):
        lowest, highest = first_tall[low : low + 32, :], last_tall[low : low + 32, :]
        for tap in range(K):
            offset = float(tap - HALF)
            masks[tap, low - first_row : low - first_row + 32, :] = jnp.where(
                (lowest <= offset) & (highest > offset), 1.0, 0.0
            ).astype(F32)
    tap_box[...] = jnp.zeros_like(tap_box)
    tap_box[0:K, 0:width] = taps[...]
    tap_box[...] = tap_box[...] + pltpu.roll(tap_box[...], 64, 1)

    edges = {}

    def rs_finish(stage, chunk, way):
        flights[stage, chunk].wait_recv()
        low, rows = starts[stage]
        if stage < 4:
            mid = rows // 2
            nxt = starts[stage + 1][0]
            rs_send[chunk, nxt : nxt + mid, :] = (
                keep[chunk, mid:rows, :] + rs_recv[chunk, low + mid : low + rows, :].astype(F32)
            ).astype(BF16)
            flights[stage + 1, chunk] = rs_start(stage + 1, chunk, way)
            keep[chunk, 0:mid, :] = keep[chunk, 0:mid, :] + rs_recv[
                chunk, low : low + mid, :
            ].astype(F32)
            return
        columns = slice(chunk * LANES, (chunk + 1) * LANES)
        branch = keep[chunk, 0:rows, :] + rs_recv[chunk, low : low + rows, :].astype(F32)
        mixed = (own[:, columns] + 0.5 * branch).astype(BF16)
        place(x_wide, chunk, mixed.astype(F32))
        if chunk == 0:
            edge_send[1] = mixed
            edges[1] = send(edge_send.at[1], edge_recv.at[1], before)
        if chunk == chunks - 1:
            edge_send[0] = mixed
            edges[0] = send(edge_send.at[0], edge_recv.at[0], after)

    for turn in range(len(units) + 4):
        for stage in range(5):
            if 0 <= turn - stage < len(units):
                for chunk, way in units[turn - stage]:
                    rs_finish(stage, chunk, way)

    for side, block in ((0, -1), (1, chunks)):
        cot_copies[side].wait_recv()
        place(cot_wide, block, cot_recv[side].astype(F32))
    turn_round(cot_wide, cot_tall)
    for side, block in ((0, -1), (1, chunks)):
        edges[side].wait_recv()
        place(x_wide, block, edge_recv[side].astype(F32))
    turn_round(x_wide, x_tall)

    spans = side_length // LANES
    step = 104
    for low in range(first_row, last_row, step):
        here = x_tall[low : low + step, :]
        conv = jnp.zeros((step, LANES), F32)
        for tap in range(K):
            moved = x_tall[low + tap - HALF : low + tap - HALF + step, :]
            mask = masks[tap, low - first_row : low - first_row + step, :]
            conv = conv + tap_box[tap : tap + 1, :] * (moved * mask)
        gate = jax.nn.sigmoid(conv)
        grad_tall[low : low + step, :] = (
            cot_tall[low : low + step, :] * gate * (1.0 + conv * (1.0 - gate))
        )
        out_tall[low : low + step, :] = here + conv * gate

    def convolve_back(unit):
        parts = []
        step = LANES // 2
        for low in range(LANES * (unit + 1), LANES * (unit + 2), step):
            here = x_tall[low : low + step, :]
            total = cot_tall[low : low + step, :]
            for tap in range(K):
                moved = grad_tall[low + HALF - tap : low + HALF - tap + step, :]
                moved = moved * masks[K - 1 - tap, low - first_row : low - first_row + step, :]
                total = total + tap_box[tap : tap + 1, :] * moved
                term = jnp.sum((moved * here).reshape(step // 8, 8, LANES), axis=0)
                if low == LANES:
                    tap_sums[tap] = term
                else:
                    tap_sums[tap] = tap_sums[tap] + term
            parts.append(total)
        return jnp.concatenate(parts, axis=0).T

    ag = {}

    def ag_start(stage, unit, way):
        first, second = WAYS[way]
        target = (z_way(first), z_way(second), x_way(first), x_way(second), sibling)[stage]
        rows = width << stage
        return send(
            gathered.at[unit, way, pl.ds(0, rows), :],
            gathered.at[unit, way, pl.ds(rows, rows), :],
            target,
        )

    for unit in range(spans):
        grad_mixed = convolve_back(unit).astype(BF16)
        for way in range(2):
            gathered[unit, way, 0:width, :] = grad_mixed[64 * way : 64 * way + width, :]
            ag[0, unit, way] = ag_start(0, unit, way)
    for unit in range(spans):
        output = out_tall[LANES * (unit + 1) : LANES * (unit + 2), :].T.astype(BF16)
        for way in range(2):
            left = side_length * way + LANES * unit
            out_t[:, left : left + LANES] = output[64 * way : 64 * way + width, :]
    tap_sums[K] = jnp.zeros((8, LANES), F32)
    sums = jnp.sum(tap_sums[...], axis=1)
    sums = sums + pltpu.roll(sums, 64, 1)
    kernel_ring[y] = sums

    taps_flight = {}

    def taps_start(hop):
        for step, hops in ((1, 4), (-1, 3)):
            if hop > hops:
                continue
            spot = lax.rem(y + NY - step * (hop - 1), NY)
            taps_flight[hop, step] = send(kernel_ring.at[spot], kernel_ring.at[spot], y_way(step))

    def taps_wait(hop):
        for step in (1, -1):
            if (hop, step) in taps_flight:
                taps_flight[hop, step].wait_recv()

    taps_start(1)

    def ag_finish(stage, unit):
        for way in range(2):
            ag[stage, unit, way].wait_recv()
            if stage < 4:
                ag[stage + 1, unit, way] = ag_start(stage + 1, unit, way)
                continue
            for c in range(2):
                for i in range(NX):
                    for j in range(NZ):
                        home = tensor_at(
                            flip(z, relative(j, way)),
                            flip(x, relative(i, way)),
                            1 - core if c else core,
                        )
                        spot = (c * NX + i) * NZ + j
                        left = side_length * way + LANES * unit
                        piece[
                            pl.ds(pl.multiple_of(home * width, 16), width), left : left + LANES
                        ] = gathered[unit, way, spot * width : (spot + 1) * width, :]

    for turn in range(spans + 4):
        for stage in range(5):
            if 0 <= turn - stage < spans:
                ag_finish(stage, turn - stage)
        if turn in (1, 2, 3):
            taps_wait(turn)
            taps_start(turn + 1)
    taps_wait(4)
    total = kernel_ring[0]
    for i in range(1, NY):
        total = total + kernel_ring[i]
    kernel_cross[w] = total
    cross = [send(kernel_cross.at[w], kernel_cross.at[w], w_way(step)) for step in (1, 2)]

    tall, broad = hid // 2, depth // 4

    def down_chunks(i):
        left = broad * i
        product = dot(hidden[...], piece[left : left + broad, :], 1, 1)
        totals[0, 2 * i], totals[0, 2 * i + 1] = product[:tall], product[tall:]

    def up_chunks(i):
        left = broad * i
        product = dot(grad_act[...], normed[:, left : left + broad], 1, 0)
        totals[1, 2 * i], totals[1, 2 * i + 1] = product[:tall], product[tall:]

    ring = {}

    def ring_spot(stream, side, k):
        return (stream * 2 + side) * 4 + k - 1

    def ring_start(stream, side, k):
        step = (1, -1)[side]
        if k > HOPS[stream][side]:
            return
        chunk = lax.rem(y + NY + step * k, NY)
        value = totals[stream, chunk]
        if k < HOPS[stream][side]:
            ring[stream, side, k + 1].wait_recv()
            value = value + ring_recv[ring_spot(stream, side, k + 1)].astype(F32)
        spot = ring_spot(stream, side, k)
        ring_send[spot] = value.astype(BF16)
        ring[stream, side, k] = send(ring_send.at[spot], ring_recv.at[spot], y_way(step))

    for i in range(4):
        down_chunks(i)
    ring_start(0, 0, 4)
    ring_start(0, 1, 3)
    grad_hidden = 0.5 * dot(w_down[...], piece[...], 1, 0)
    gate = sig[...]
    grad_act[...] = (grad_hidden * gate * (1.0 + act[...] * (1.0 - gate))).astype(BF16)
    for i in range(4):
        up_chunks(i)
    ring_start(1, 1, 4)
    ring_start(1, 0, 3)
    ring_start(0, 0, 3)
    ring_start(1, 1, 3)
    for k in (2, 1):
        ring_start(0, 1, k)
        ring_start(1, 0, k)
        ring_start(0, 0, k)
        ring_start(1, 1, k)

    third = tall // NW
    cross_flight = {}
    for stream in range(2):
        for side in range(2):
            ring[stream, side, 1].wait_recv()
        totals[stream, y] = (
            totals[stream, y]
            + ring_recv[ring_spot(stream, 0, 1)].astype(F32)
            + ring_recv[ring_spot(stream, 1, 1)].astype(F32)
        )
        for step in (1, 2):
            rows = pl.ds(pl.multiple_of(lax.rem(w + step, NW) * third, third), third)
            cross_send[stream * 2 + step - 1] = totals[stream, y, rows, :].astype(BF16)
            cross_flight[stream, step] = send(
                cross_send.at[stream * 2 + step - 1],
                cross_recv.at[stream * 2 + step - 1],
                w_way(step),
            )
    for copy in cross:
        copy.wait_recv()
    scale = 1.0 / math.sqrt(length * count)
    summed = (kernel_cross[0] + kernel_cross[1] + kernel_cross[2]) * scale
    kernel_sum[...] = summed[0:K, 0:width]
    mine = pl.ds(pl.multiple_of(w * third, third), third)
    share = {}
    for stream in range(2):
        value = totals[stream, y, mine, :]
        for step in (1, 2):
            cross_flight[stream, step].wait_recv()
            value = value + cross_recv[stream * 2 + step - 1].astype(F32)
        whole[stream, y, mine, :] = value.astype(BF16)
        for step in (1, 2):
            share[stream, step] = send(
                whole.at[stream, y, mine, :], whole.at[stream, y, mine, :], w_way(step)
            )
    spread = {}
    for k in range(1, 6):
        for stream in range(2):
            if k == 1:
                for step in (1, 2):
                    share[stream, step].wait_recv()
            for side in range(2):
                step = (1, -1)[side]
                if 1 < k <= HOPS[stream][side] + 1:
                    spread[stream, side, k - 1].wait_recv()
                if k <= HOPS[stream][side]:
                    spot = lax.rem(y + NY - step * (k - 1), NY)
                    spread[stream, side, k] = send(
                        whole.at[stream, spot], whole.at[stream, spot], y_way(step)
                    )
    for stream in range(2):
        for d in range(8):
            low, left = tall * (d % 2), broad * (d // 2)
            grads[stream, low : low + tall, left : left + broad] = whole[stream, d]
    for copy in started:
        copy.wait_send()


def body(frames, w_up, w_down, taps, bounds, cot):
    length, depth = frames.shape
    width = taps.shape[1]
    hid = w_up.shape[1]
    ext = length // 2 + 2 * LANES
    chunks = length // LANES
    rs_rows = depth // 2 + depth // 4 + depth // 8 + depth // 16 + depth // 32
    block = (hid // 2, depth // 4)
    vmem = pl.BlockSpec(memory_space=pltpu.VMEM)
    out_t, kernel_sum, grads = pl.pallas_call(
        kernel,
        out_shape=(
            jax.ShapeDtypeStruct((width, length), BF16),
            jax.ShapeDtypeStruct((K, width), F32),
            jax.ShapeDtypeStruct((2, hid, depth), BF16),
        ),
        in_specs=[vmem] * 6,
        out_specs=(vmem,) * 3,
        scratch_shapes=[
            pltpu.VMEM((length, depth), BF16),
            pltpu.VMEM((depth, hid), BF16),
            pltpu.VMEM((2, depth, hid), BF16),
            pltpu.VMEM((hid, length), F32),
            pltpu.VMEM((hid, length), F32),
            pltpu.VMEM((hid, length), BF16),
            pltpu.VMEM((chunks, depth // 2, LANES), F32),
            pltpu.VMEM((chunks, rs_rows, LANES), BF16),
            pltpu.VMEM((chunks, rs_rows, LANES), BF16),
            pltpu.VMEM((width, length), F32),
            pltpu.VMEM((LANES, ext), F32),
            pltpu.VMEM((LANES, ext), F32),
            pltpu.VMEM((ext, LANES), F32),
            pltpu.VMEM((ext, LANES), F32),
            pltpu.VMEM((ext, LANES), F32),
            pltpu.VMEM((ext, LANES), F32),
            pltpu.VMEM((ext, LANES), F32),
            pltpu.VMEM((ext, LANES), F32),
            pltpu.VMEM((2, width, LANES), BF16),
            pltpu.VMEM((2, width, LANES), BF16),
            pltpu.VMEM((2, width, LANES), BF16),
            pltpu.VMEM((2, width, LANES), BF16),
            pltpu.VMEM((K, length // 2 + 32, LANES), F32),
            pltpu.VMEM((K + 1, LANES), F32),
            pltpu.VMEM((K + 1, 8, LANES), F32),
            pltpu.VMEM((chunks // 2, 2, depth, LANES), BF16),
            pltpu.VMEM((depth, length), BF16),
            pltpu.VMEM((hid, length), BF16),
            pltpu.VMEM((2, NY, *block), F32),
            pltpu.VMEM((16, *block), BF16),
            pltpu.VMEM((16, *block), BF16),
            pltpu.VMEM((4, block[0] // NW, block[1]), BF16),
            pltpu.VMEM((4, block[0] // NW, block[1]), BF16),
            pltpu.VMEM((2, NY, *block), BF16),
            pltpu.VMEM((NY, K + 1, LANES), F32),
            pltpu.VMEM((NW, K + 1, LANES), F32),
            pltpu.SemaphoreType.DMA((COPIES,)),
            pltpu.SemaphoreType.DMA((COPIES,)),
        ],
        compiler_params=pltpu.CompilerParams(
            collective_id=0, has_side_effects=True, vmem_limit_bytes=60 << 20
        ),
    )(frames, w_up.T, w_down, taps, bounds, cot.T)
    scale = 1.0 / math.sqrt(length * NY * NW)
    down, up = grads[0].astype(F32) * (0.5 * scale), grads[1].astype(F32) * scale
    return out_t.T, up.T, down, kernel_sum


def solution(mesh):
    return jax.shard_map(
        body,
        mesh=mesh,
        in_specs=(
            P("seq", None),
            P(None, "tensor"),
            P("tensor", None),
            P(None, "tensor"),
            P(None, "seq"),
            P("seq", "tensor"),
        ),
        out_specs=(P("seq", "tensor"), P(None, "tensor"), P("tensor", None), P(None, "tensor")),
        check_vma=False,
    )
```

```python
import math
from functools import partial

import jax
import jax.numpy as jnp
from jax import lax
from jax.experimental import pallas as pl
from jax.experimental.pallas import tpu as pltpu
from jax.sharding import PartitionSpec as P

MESH = pl.DeviceIdType.MESH
K = 31
HALF = K // 2
NY, NW, NZ, NX = 8, 3, 4, 4
LANES = 128
WAYS = ((1, 3), (3, 1))
HOPS = ((4, 3), (3, 4))
COPIES = 137
F32, BF16 = jnp.float32, jnp.bfloat16


def flip(index, mask):
    if mask == 0:
        return index
    if mask == 1:
        return index + 1 - 2 * lax.rem(index, 2)
    if mask == 2:
        return lax.rem(index + 2, 4)
    return 3 - index


def relative(place, way):
    first, second = WAYS[way]
    return (first if place & 1 else 0) ^ (second if place & 2 else 0)


def dot(a, b, a_dim, b_dim):
    return lax.dot_general(a, b, (((a_dim,), (b_dim,)), ((), ())), preferred_element_type=F32)


def kernel(
    frames,
    w_up_t,
    w_down,
    taps,
    bounds,
    cot_t,
    out_t,
    kernel_sum,
    grads,
    normed,
    w_down_t,
    ordered,
    act,
    sig,
    hidden,
    keep,
    rs_send,
    rs_recv,
    own,
    x_wide,
    cot_wide,
    x_tall,
    cot_tall,
    grad_tall,
    out_tall,
    first_tall,
    last_tall,
    edge_send,
    edge_recv,
    cot_send,
    cot_recv,
    masks,
    tap_box,
    tap_sums,
    gathered,
    piece,
    grad_act,
    totals,
    ring_send,
    ring_recv,
    cross_send,
    cross_recv,
    whole,
    kernel_ring,
    kernel_cross,
    send_sems,
    recv_sems,
):
    length, depth = frames.shape
    width = taps.shape[1]
    hid = w_up_t.shape[0]
    side_length = length // 2
    ext = side_length + 2 * LANES
    seq, ten = lax.axis_index("seq"), lax.axis_index("tensor")
    y, w = lax.div(seq, NW), lax.rem(seq, NW)
    core, x, z = lax.rem(ten, 2), lax.rem(lax.div(ten, 2), NX), lax.div(ten, 2 * NX)

    def tensor_at(z, x, core):
        return (z * NX + x) * 2 + core

    def x_way(mask):
        return (seq, tensor_at(z, flip(x, mask), core))

    def z_way(mask):
        return (seq, tensor_at(flip(z, mask), x, core))

    def y_way(step):
        return (lax.rem(y + NY + step, NY) * NW + w, ten)

    def w_way(step):
        return (y * NW + lax.rem(w + step, NW), ten)

    sibling = (seq, tensor_at(z, x, 1 - core))
    count = NY * NW
    after = (lax.rem(seq + 1, count), ten)
    before = (lax.rem(seq + count - 1, count), ten)

    barrier = pltpu.get_barrier_semaphore()
    partners = [sibling, x_way(1), x_way(3), z_way(1), z_way(3), after, before]
    partners += [y_way(1), y_way(-1), w_way(1), w_way(2)]
    for partner in partners:
        pl.semaphore_signal(barrier, inc=1, device_id=partner, device_id_type=MESH)

    started = []

    def send(src, dst, target):
        spot = len(started)
        copy = pltpu.make_async_remote_copy(
            src_ref=src,
            dst_ref=dst,
            send_sem=send_sems.at[spot],
            recv_sem=recv_sems.at[spot],
            device_id=target,
            device_id_type=MESH,
        )
        copy.start()
        started.append(copy)
        return copy

    w_down_t[...] = w_down[...].astype(F32).T.astype(BF16)
    for way in range(2):
        for c in range(2):
            for i in range(NX):
                for j in range(NZ):
                    home = tensor_at(
                        flip(z, relative(j, way)),
                        flip(x, relative(i, way)),
                        1 - core if c else core,
                    )
                    spot = (c * NX + i) * NZ + j
                    ordered[way, spot * width : (spot + 1) * width, :] = w_down_t[
                        pl.ds(pl.multiple_of(home * width, 16), width), :
                    ]
    cot_send[0] = cot_t[:, length - LANES :]
    cot_send[1] = cot_t[:, :LANES]

    half = depth // 2
    starts, height = [], half
    offset = 0
    for _ in range(5):
        starts.append((offset, height))
        offset += height
        height //= 2
    chunks = length // LANES
    units = [((i, 0), (chunks - 1 - i, 1)) for i in range(chunks // 2)]

    def rs_start(stage, chunk, way):
        first, second = WAYS[way]
        target = (sibling, x_way(second), x_way(first), z_way(second), z_way(first))[stage]
        low, rows = starts[stage]
        return send(
            rs_send.at[chunk, pl.ds(low, rows), :], rs_recv.at[chunk, pl.ds(low, rows), :], target
        )

    flights = {}
    cot_copies = []
    first_row, last_row = LANES - 16, LANES + side_length + 16

    def place(wide, block, value):
        if block <= ext // LANES - 2:
            wide[0:width, (block + 1) * LANES : (block + 2) * LANES] = value
        shifted = block - side_length // LANES
        if shifted >= -1:
            wide[64 : 64 + width, (shifted + 1) * LANES : (shifted + 2) * LANES] = value

    def turn_round(wide, tall):
        for low in range(0, ext, LANES):
            tall[low : low + LANES, :] = wide[:, low : low + LANES].T

    def hidden_chunk(chunk):
        rows = slice(chunk * LANES, (chunk + 1) * LANES)
        wide = frames[rows, :].astype(F32)
        mean = jnp.mean(wide, axis=1, keepdims=True)
        centred = wide - mean
        var = jnp.mean(centred * centred, axis=1, keepdims=True)
        normed[rows, :] = (centred / jnp.sqrt(var + 1e-05)).astype(BF16)
        up = dot(w_up_t[...], normed[rows, :], 1, 1)
        gate = jax.nn.sigmoid(up)
        act[:, rows] = up
        sig[:, rows] = gate
        hidden[:, rows] = (up * gate).astype(BF16)

    def rs_begin(turn):
        unit = units[turn]
        for chunk, _ in unit:
            hidden_chunk(chunk)
        if turn == 0:
            pl.semaphore_wait(barrier, len(partners))
        for chunk, way in unit:
            part = hidden[:, chunk * LANES : (chunk + 1) * LANES]
            rs_send[chunk, 0:half, :] = dot(ordered[way, half:, :], part, 1, 0).astype(BF16)
            flights[0, chunk] = rs_start(0, chunk, way)
        for chunk, way in unit:
            part = hidden[:, chunk * LANES : (chunk + 1) * LANES]
            keep[chunk] = dot(ordered[way, :half, :], part, 1, 0)

    def prepare_masks():
        limits = bounds[...]
        limits = jnp.concatenate(
            [
                jnp.broadcast_to(limits[:, :1], (2, LANES)),
                limits,
                jnp.broadcast_to(limits[:, length - 1 :], (2, LANES)),
            ],
            axis=1,
        )
        spots = seq * length - LANES + lax.broadcasted_iota(jnp.int32, limits.shape, 1)
        limits = (limits - spots).astype(F32)
        for row, tall in ((0, first_tall), (1, last_tall)):
            for low in range(0, ext, LANES):
                tall[low : low + LANES, :] = jnp.concatenate(
                    [
                        jnp.broadcast_to(limits[row : row + 1, low + i : low + i + LANES], (64, LANES))
                        for i in (0, side_length)
                    ],
                    axis=0,
                ).T
        for low in range(first_row, last_row, 32):
            lowest, highest = first_tall[low : low + 32, :], last_tall[low : low + 32, :]
            for tap in range(K):
                offset = float(tap - HALF)
                masks[tap, low - first_row : low - first_row + 32, :] = jnp.where(
                    (lowest <= offset) & (highest > offset), 1.0, 0.0
                ).astype(F32)

    def prepare_taps():
        x_wide[...] = jnp.zeros_like(x_wide)
        cot_wide[...] = jnp.zeros_like(cot_wide)
        for block in range(chunks):
            place(cot_wide, block, cot_t[:, block * LANES : (block + 1) * LANES].astype(F32))
        tap_box[...] = jnp.zeros_like(tap_box)
        tap_box[0:K, 0:width] = taps[...]
        tap_box[...] = tap_box[...] + pltpu.roll(tap_box[...], 64, 1)

    def prepare_own():
        pick = (
            lax.broadcasted_iota(jnp.int32, (width, depth), 1)
            == ten * width + lax.broadcasted_iota(jnp.int32, (width, depth), 0)
        ).astype(BF16)
        own[...] = dot(pick, frames[...], 1, 1)

    edges = {}

    def rs_finish(stage, chunk, way):
        flights[stage, chunk].wait_recv()
        low, rows = starts[stage]
        if stage < 4:
            mid = rows // 2
            nxt = starts[stage + 1][0]
            rs_send[chunk, nxt : nxt + mid, :] = (
                keep[chunk, mid:rows, :] + rs_recv[chunk, low + mid : low + rows, :].astype(F32)
            ).astype(BF16)
            flights[stage + 1, chunk] = rs_start(stage + 1, chunk, way)
            keep[chunk, 0:mid, :] = keep[chunk, 0:mid, :] + rs_recv[
                chunk, low : low + mid, :
            ].astype(F32)
            return
        columns = slice(chunk * LANES, (chunk + 1) * LANES)
        branch = keep[chunk, 0:rows, :] + rs_recv[chunk, low : low + rows, :].astype(F32)
        mixed = (own[:, columns] + 0.5 * branch).astype(BF16)
        place(x_wide, chunk, mixed.astype(F32))
        if chunk == 0:
            edge_send[1] = mixed
            edges[1] = send(edge_send.at[1], edge_recv.at[1], before)
        if chunk == chunks - 1:
            edge_send[0] = mixed
            edges[0] = send(edge_send.at[0], edge_recv.at[0], after)

    for turn in range(len(units) + 5):
        if turn < len(units):
            rs_begin(turn)
        for stage in range(5):
            if 0 <= turn - 1 - stage < len(units):
                for chunk, way in units[turn - 1 - stage]:
                    rs_finish(stage, chunk, way)
        if turn == 1:
            cot_copies.append(send(cot_send.at[0], cot_recv.at[0], after))
            cot_copies.append(send(cot_send.at[1], cot_recv.at[1], before))
            prepare_taps()
        if turn == 2:
            prepare_own()
        if turn == 3:
            prepare_masks()

    for side, block in ((0, -1), (1, chunks)):
        cot_copies[side].wait_recv()
        place(cot_wide, block, cot_recv[side].astype(F32))
    turn_round(cot_wide, cot_tall)
    for side, block in ((0, -1), (1, chunks)):
        edges[side].wait_recv()
        place(x_wide, block, edge_recv[side].astype(F32))
    turn_round(x_wide, x_tall)

    spans = side_length // LANES
    step = 104
    for low in range(first_row, last_row, step):
        here = x_tall[low : low + step, :]
        conv = jnp.zeros((step, LANES), F32)
        for tap in range(K):
            moved = x_tall[low + tap - HALF : low + tap - HALF + step, :]
            mask = masks[tap, low - first_row : low - first_row + step, :]
            conv = conv + tap_box[tap : tap + 1, :] * (moved * mask)
        gate = jax.nn.sigmoid(conv)
        grad_tall[low : low + step, :] = (
            cot_tall[low : low + step, :] * gate * (1.0 + conv * (1.0 - gate))
        )
        out_tall[low : low + step, :] = here + conv * gate

    def convolve_back(unit):
        parts = []
        step = LANES // 2
        for low in range(LANES * (unit + 1), LANES * (unit + 2), step):
            here = x_tall[low : low + step, :]
            total = cot_tall[low : low + step, :]
            for tap in range(K):
                moved = grad_tall[low + HALF - tap : low + HALF - tap + step, :]
                moved = moved * masks[K - 1 - tap, low - first_row : low - first_row + step, :]
                total = total + tap_box[tap : tap + 1, :] * moved
                term = jnp.sum((moved * here).reshape(step // 8, 8, LANES), axis=0)
                if low == LANES:
                    tap_sums[tap] = term
                else:
                    tap_sums[tap] = tap_sums[tap] + term
            parts.append(total)
        return jnp.concatenate(parts, axis=0).T

    ag = {}

    def ag_start(stage, unit, way):
        first, second = WAYS[way]
        target = (z_way(first), z_way(second), x_way(first), x_way(second), sibling)[stage]
        rows = width << stage
        return send(
            gathered.at[unit, way, pl.ds(0, rows), :],
            gathered.at[unit, way, pl.ds(rows, rows), :],
            target,
        )

    for unit in range(spans):
        grad_mixed = convolve_back(unit).astype(BF16)
        for way in range(2):
            gathered[unit, way, 0:width, :] = grad_mixed[64 * way : 64 * way + width, :]
            ag[0, unit, way] = ag_start(0, unit, way)
    for unit in range(spans):
        output = out_tall[LANES * (unit + 1) : LANES * (unit + 2), :].T.astype(BF16)
        for way in range(2):
            left = side_length * way + LANES * unit
            out_t[:, left : left + LANES] = output[64 * way : 64 * way + width, :]
    tap_sums[K] = jnp.zeros((8, LANES), F32)
    sums = jnp.sum(tap_sums[...], axis=1)
    sums = sums + pltpu.roll(sums, 64, 1)
    kernel_ring[y] = sums

    taps_flight = {}

    def taps_start(hop):
        for step, hops in ((1, 4), (-1, 3)):
            if hop > hops:
                continue
            spot = lax.rem(y + NY - step * (hop - 1), NY)
            taps_flight[hop, step] = send(kernel_ring.at[spot], kernel_ring.at[spot], y_way(step))

    def taps_wait(hop):
        for step in (1, -1):
            if (hop, step) in taps_flight:
                taps_flight[hop, step].wait_recv()

    taps_start(1)

    def ag_finish(stage, unit):
        for way in range(2):
            ag[stage, unit, way].wait_recv()
            if stage < 4:
                ag[stage + 1, unit, way] = ag_start(stage + 1, unit, way)
                continue
            for c in range(2):
                for i in range(NX):
                    for j in range(NZ):
                        home = tensor_at(
                            flip(z, relative(j, way)),
                            flip(x, relative(i, way)),
                            1 - core if c else core,
                        )
                        spot = (c * NX + i) * NZ + j
                        left = side_length * way + LANES * unit
                        piece[
                            pl.ds(pl.multiple_of(home * width, 16), width), left : left + LANES
                        ] = gathered[unit, way, spot * width : (spot + 1) * width, :]

    for turn in range(spans + 4):
        for stage in range(5):
            if 0 <= turn - stage < spans:
                ag_finish(stage, turn - stage)
        if turn in (1, 2, 3):
            taps_wait(turn)
            taps_start(turn + 1)
    taps_wait(4)
    total = kernel_ring[0]
    for i in range(1, NY):
        total = total + kernel_ring[i]
    kernel_cross[w] = total
    cross = [send(kernel_cross.at[w], kernel_cross.at[w], w_way(step)) for step in (1, 2)]

    tall, broad = hid // 2, depth // 4

    def down_chunks(i):
        left = broad * i
        product = dot(hidden[...], piece[left : left + broad, :], 1, 1)
        totals[0, 2 * i], totals[0, 2 * i + 1] = product[:tall], product[tall:]

    def up_chunks(i):
        left = broad * i
        product = dot(grad_act[...], normed[:, left : left + broad], 1, 0)
        totals[1, 2 * i], totals[1, 2 * i + 1] = product[:tall], product[tall:]

    ring = {}

    def ring_spot(stream, side, k):
        return (stream * 2 + side) * 4 + k - 1

    def ring_start(stream, side, k):
        step = (1, -1)[side]
        if k > HOPS[stream][side]:
            return
        chunk = lax.rem(y + NY + step * k, NY)
        value = totals[stream, chunk]
        if k < HOPS[stream][side]:
            ring[stream, side, k + 1].wait_recv()
            value = value + ring_recv[ring_spot(stream, side, k + 1)].astype(F32)
        spot = ring_spot(stream, side, k)
        ring_send[spot] = value.astype(BF16)
        ring[stream, side, k] = send(ring_send.at[spot], ring_recv.at[spot], y_way(step))

    for i in range(4):
        down_chunks(i)
    ring_start(0, 0, 4)
    ring_start(0, 1, 3)
    grad_hidden = 0.5 * dot(w_down[...], piece[...], 1, 0)
    gate = sig[...]
    grad_act[...] = (grad_hidden * gate * (1.0 + act[...] * (1.0 - gate))).astype(BF16)
    for i in range(4):
        up_chunks(i)
    ring_start(1, 1, 4)
    ring_start(1, 0, 3)
    ring_start(0, 0, 3)
    ring_start(1, 1, 3)
    for k in (2, 1):
        ring_start(0, 1, k)
        ring_start(1, 0, k)
        ring_start(0, 0, k)
        ring_start(1, 1, k)

    third = tall // NW
    cross_flight = {}
    for stream in range(2):
        for side in range(2):
            ring[stream, side, 1].wait_recv()
        totals[stream, y] = (
            totals[stream, y]
            + ring_recv[ring_spot(stream, 0, 1)].astype(F32)
            + ring_recv[ring_spot(stream, 1, 1)].astype(F32)
        )
        for step in (1, 2):
            rows = pl.ds(pl.multiple_of(lax.rem(w + step, NW) * third, third), third)
            cross_send[stream * 2 + step - 1] = totals[stream, y, rows, :].astype(BF16)
            cross_flight[stream, step] = send(
                cross_send.at[stream * 2 + step - 1],
                cross_recv.at[stream * 2 + step - 1],
                w_way(step),
            )
    for copy in cross:
        copy.wait_recv()
    scale = 1.0 / math.sqrt(length * count)
    summed = (kernel_cross[0] + kernel_cross[1] + kernel_cross[2]) * scale
    kernel_sum[...] = summed[0:K, 0:width]
    mine = pl.ds(pl.multiple_of(w * third, third), third)
    share = {}
    for stream in range(2):
        value = totals[stream, y, mine, :]
        for step in (1, 2):
            cross_flight[stream, step].wait_recv()
            value = value + cross_recv[stream * 2 + step - 1].astype(F32)
        whole[stream, y, mine, :] = value.astype(BF16)
        for step in (1, 2):
            share[stream, step] = send(
                whole.at[stream, y, mine, :], whole.at[stream, y, mine, :], w_way(step)
            )
    spread = {}
    for k in range(1, 6):
        for part in range(NW):
            rows = pl.ds(pl.multiple_of(lax.rem(w + NW - part, NW) * third, third), third)
            for stream in range(2):
                if k == 1 and part > 0:
                    share[stream, part].wait_recv()
                for side in range(2):
                    step = (1, -1)[side]
                    if 1 < k <= HOPS[stream][side] + 1:
                        spread[stream, side, k - 1, part].wait_recv()
                    if k <= HOPS[stream][side]:
                        spot = lax.rem(y + NY - step * (k - 1), NY)
                        spread[stream, side, k, part] = send(
                            whole.at[stream, spot, rows, :],
                            whole.at[stream, spot, rows, :],
                            y_way(step),
                        )
    for stream in range(2):
        for d in range(8):
            low, left = tall * (d % 2), broad * (d // 2)
            grads[stream, low : low + tall, left : left + broad] = whole[stream, d]
    for copy in started:
        copy.wait_send()


def finish(scale, grads, out_t, kernel_sum, down, up_t, out, kernel_out):
    down[...] = grads[0].astype(F32) * (0.5 * scale)
    up_t[...] = grads[1].astype(F32) * scale
    out[...] = out_t[...]
    kernel_out[...] = kernel_sum[...]


def body(frames, w_up, w_down, taps, bounds, cot):
    length, depth = frames.shape
    width = taps.shape[1]
    hid = w_up.shape[1]
    ext = length // 2 + 2 * LANES
    chunks = length // LANES
    rs_rows = depth // 2 + depth // 4 + depth // 8 + depth // 16 + depth // 32
    block = (hid // 2, depth // 4)
    vmem = pl.BlockSpec(memory_space=pltpu.VMEM)
    out_t, kernel_sum, grads = pl.pallas_call(
        kernel,
        out_shape=(
            jax.ShapeDtypeStruct((width, length), BF16),
            jax.ShapeDtypeStruct((K, width), F32),
            jax.ShapeDtypeStruct((2, hid, depth), BF16),
        ),
        in_specs=[vmem] * 6,
        out_specs=(vmem,) * 3,
        scratch_shapes=[
            pltpu.VMEM((length, depth), BF16),
            pltpu.VMEM((depth, hid), BF16),
            pltpu.VMEM((2, depth, hid), BF16),
            pltpu.VMEM((hid, length), F32),
            pltpu.VMEM((hid, length), F32),
            pltpu.VMEM((hid, length), BF16),
            pltpu.VMEM((chunks, depth // 2, LANES), F32),
            pltpu.VMEM((chunks, rs_rows, LANES), BF16),
            pltpu.VMEM((chunks, rs_rows, LANES), BF16),
            pltpu.VMEM((width, length), F32),
            pltpu.VMEM((LANES, ext), F32),
            pltpu.VMEM((LANES, ext), F32),
            pltpu.VMEM((ext, LANES), F32),
            pltpu.VMEM((ext, LANES), F32),
            pltpu.VMEM((ext, LANES), F32),
            pltpu.VMEM((ext, LANES), F32),
            pltpu.VMEM((ext, LANES), F32),
            pltpu.VMEM((ext, LANES), F32),
            pltpu.VMEM((2, width, LANES), BF16),
            pltpu.VMEM((2, width, LANES), BF16),
            pltpu.VMEM((2, width, LANES), BF16),
            pltpu.VMEM((2, width, LANES), BF16),
            pltpu.VMEM((K, length // 2 + 32, LANES), F32),
            pltpu.VMEM((K + 1, LANES), F32),
            pltpu.VMEM((K + 1, 8, LANES), F32),
            pltpu.VMEM((chunks // 2, 2, depth, LANES), BF16),
            pltpu.VMEM((depth, length), BF16),
            pltpu.VMEM((hid, length), BF16),
            pltpu.VMEM((2, NY, *block), F32),
            pltpu.VMEM((16, *block), BF16),
            pltpu.VMEM((16, *block), BF16),
            pltpu.VMEM((4, block[0] // NW, block[1]), BF16),
            pltpu.VMEM((4, block[0] // NW, block[1]), BF16),
            pltpu.VMEM((2, NY, *block), BF16),
            pltpu.VMEM((NY, K + 1, LANES), F32),
            pltpu.VMEM((NW, K + 1, LANES), F32),
            pltpu.SemaphoreType.DMA((COPIES,)),
            pltpu.SemaphoreType.DMA((COPIES,)),
        ],
        compiler_params=pltpu.CompilerParams(
            collective_id=0, has_side_effects=True, vmem_limit_bytes=60 << 20
        ),
    )(frames, w_up.T, w_down, taps, bounds, cot.T)
    scale = 1.0 / math.sqrt(length * NY * NW)
    steps = 4
    rows = pl.BlockSpec((hid // steps, depth), lambda i: (i, 0))
    out_all = pl.BlockSpec((width, length), lambda i: (0, 0))
    taps_all = pl.BlockSpec((K, width), lambda i: (0, 0))
    down, up_t, out_t, kernel_sum = pl.pallas_call(
        partial(finish, scale),
        grid=(steps,),
        out_shape=(
            jax.ShapeDtypeStruct((hid, depth), F32),
            jax.ShapeDtypeStruct((hid, depth), F32),
            jax.ShapeDtypeStruct((width, length), BF16),
            jax.ShapeDtypeStruct((K, width), F32),
        ),
        in_specs=[
            pl.BlockSpec((2, hid // steps, depth), lambda i: (0, i, 0)),
            out_all,
            taps_all,
        ],
        out_specs=(rows, rows, out_all, taps_all),
    )(grads, out_t, kernel_sum)
    return out_t.T, up_t.T, down, kernel_sum


def solution(mesh):
    return jax.shard_map(
        body,
        mesh=mesh,
        in_specs=(
            P("seq", None),
            P(None, "tensor"),
            P("tensor", None),
            P(None, "tensor"),
            P(None, "seq"),
            P("seq", "tensor"),
        ),
        out_specs=(P("seq", "tensor"), P(None, "tensor"), P("tensor", None), P(None, "tensor")),
        check_vma=False,
    )
```

```python
import math
from functools import partial

import jax
import jax.numpy as jnp
from jax import lax
from jax.experimental import pallas as pl
from jax.experimental.pallas import tpu as pltpu
from jax.sharding import PartitionSpec as P

MESH = pl.DeviceIdType.MESH
K = 31
HALF = K // 2
NY, NW, NZ, NX = 8, 3, 4, 4
LANES = 128
WAYS = ((1, 3), (3, 1))
HOPS = ((4, 3), (3, 4))
COPIES = 143
F32, BF16 = jnp.float32, jnp.bfloat16


def flip(index, mask):
    if mask == 0:
        return index
    if mask == 1:
        return index + 1 - 2 * lax.rem(index, 2)
    if mask == 2:
        return lax.rem(index + 2, 4)
    return 3 - index


def relative(place, way):
    first, second = WAYS[way]
    return (first if place & 1 else 0) ^ (second if place & 2 else 0)


def dot(a, b, a_dim, b_dim):
    return lax.dot_general(a, b, (((a_dim,), (b_dim,)), ((), ())), preferred_element_type=F32)


def kernel(
    frames,
    w_up_t,
    w_down,
    taps,
    bounds,
    cot_t,
    out_t,
    kernel_sum,
    grads,
    normed,
    w_down_t,
    ordered,
    act,
    sig,
    hidden,
    keep,
    rs_send,
    rs_recv,
    own,
    x_wide,
    cot_wide,
    x_tall,
    cot_tall,
    grad_tall,
    out_tall,
    first_tall,
    last_tall,
    edge_send,
    edge_recv,
    cot_send,
    cot_recv,
    masks,
    tap_box,
    tap_sums,
    gathered,
    piece,
    totals,
    ring_send,
    ring_recv,
    cross_send,
    cross_recv,
    whole,
    kernel_ring,
    kernel_cross,
    send_sems,
    recv_sems,
):
    length, depth = frames.shape
    width = taps.shape[1]
    hid = w_up_t.shape[0]
    side_length = length // 2
    ext = side_length + 2 * LANES
    seq, ten = lax.axis_index("seq"), lax.axis_index("tensor")
    y, w = lax.div(seq, NW), lax.rem(seq, NW)
    core, x, z = lax.rem(ten, 2), lax.rem(lax.div(ten, 2), NX), lax.div(ten, 2 * NX)

    def tensor_at(z, x, core):
        return (z * NX + x) * 2 + core

    def x_way(mask):
        return (seq, tensor_at(z, flip(x, mask), core))

    def z_way(mask):
        return (seq, tensor_at(flip(z, mask), x, core))

    def y_way(step):
        return (lax.rem(y + NY + step, NY) * NW + w, ten)

    def w_way(step):
        return (y * NW + lax.rem(w + step, NW), ten)

    sibling = (seq, tensor_at(z, x, 1 - core))
    count = NY * NW
    after = (lax.rem(seq + 1, count), ten)
    before = (lax.rem(seq + count - 1, count), ten)

    barrier = pltpu.get_barrier_semaphore()
    partners = [sibling, x_way(1), x_way(3), z_way(1), z_way(3), after, before]
    partners += [y_way(1), y_way(-1), w_way(1), w_way(2)]
    for partner in partners:
        pl.semaphore_signal(barrier, inc=1, device_id=partner, device_id_type=MESH)

    started = []

    def send(src, dst, target):
        spot = len(started)
        copy = pltpu.make_async_remote_copy(
            src_ref=src,
            dst_ref=dst,
            send_sem=send_sems.at[spot],
            recv_sem=recv_sems.at[spot],
            device_id=target,
            device_id_type=MESH,
        )
        copy.start()
        started.append(copy)
        return copy

    w_down_t[...] = w_down[...].astype(F32).T.astype(BF16)
    for way in range(2):
        for c in range(2):
            for i in range(NX):
                for j in range(NZ):
                    home = tensor_at(
                        flip(z, relative(j, way)),
                        flip(x, relative(i, way)),
                        1 - core if c else core,
                    )
                    spot = (c * NX + i) * NZ + j
                    ordered[way, spot * width : (spot + 1) * width, :] = w_down_t[
                        pl.ds(pl.multiple_of(home * width, 16), width), :
                    ]
    cot_send[0] = cot_t[:, length - LANES :]
    cot_send[1] = cot_t[:, :LANES]

    half = depth // 2
    starts, height = [], half
    offset = 0
    for _ in range(5):
        starts.append((offset, height))
        offset += height
        height //= 2
    chunks = length // LANES
    units = [((i, 0), (chunks - 1 - i, 1)) for i in range(chunks // 2)]

    def rs_start(stage, chunk, way):
        first, second = WAYS[way]
        target = (sibling, x_way(second), x_way(first), z_way(second), z_way(first))[stage]
        low, rows = starts[stage]
        return send(
            rs_send.at[chunk, pl.ds(low, rows), :], rs_recv.at[chunk, pl.ds(low, rows), :], target
        )

    flights = {}
    cot_copies = []
    first_row, last_row = LANES - 16, LANES + side_length + 16

    def place(wide, block, value):
        if block <= ext // LANES - 2:
            wide[0:width, (block + 1) * LANES : (block + 2) * LANES] = value
        shifted = block - side_length // LANES
        if shifted >= -1:
            wide[64 : 64 + width, (shifted + 1) * LANES : (shifted + 2) * LANES] = value

    def turn_round(wide, tall):
        for low in range(0, ext, LANES):
            tall[low : low + LANES, :] = wide[:, low : low + LANES].T

    def hidden_chunk(chunk):
        rows = slice(chunk * LANES, (chunk + 1) * LANES)
        wide = frames[rows, :].astype(F32)
        mean = jnp.mean(wide, axis=1, keepdims=True)
        centred = wide - mean
        var = jnp.mean(centred * centred, axis=1, keepdims=True)
        normed[rows, :] = (centred / jnp.sqrt(var + 1e-05)).astype(BF16)
        up = dot(w_up_t[...], normed[rows, :], 1, 1)
        gate = jax.nn.sigmoid(up)
        act[:, rows] = up
        sig[:, rows] = gate
        hidden[:, rows] = (up * gate).astype(BF16)

    def rs_begin(turn):
        unit = units[turn]
        for chunk, _ in unit:
            hidden_chunk(chunk)
        if turn == 0:
            pl.semaphore_wait(barrier, len(partners))
        for chunk, way in unit:
            part = hidden[:, chunk * LANES : (chunk + 1) * LANES]
            rs_send[chunk, 0:half, :] = dot(ordered[way, half:, :], part, 1, 0).astype(BF16)
            flights[0, chunk] = rs_start(0, chunk, way)
        for chunk, way in unit:
            part = hidden[:, chunk * LANES : (chunk + 1) * LANES]
            keep[chunk] = dot(ordered[way, :half, :], part, 1, 0)

    def prepare_masks():
        limits = bounds[...]
        limits = jnp.concatenate(
            [
                jnp.broadcast_to(limits[:, :1], (2, LANES)),
                limits,
                jnp.broadcast_to(limits[:, length - 1 :], (2, LANES)),
            ],
            axis=1,
        )
        spots = seq * length - LANES + lax.broadcasted_iota(jnp.int32, limits.shape, 1)
        limits = (limits - spots).astype(F32)
        for row, tall in ((0, first_tall), (1, last_tall)):
            for low in range(0, ext, LANES):
                tall[low : low + LANES, :] = jnp.concatenate(
                    [
                        jnp.broadcast_to(limits[row : row + 1, low + i : low + i + LANES], (64, LANES))
                        for i in (0, side_length)
                    ],
                    axis=0,
                ).T
        for low in range(first_row, last_row, 32):
            lowest, highest = first_tall[low : low + 32, :], last_tall[low : low + 32, :]
            for tap in range(K):
                offset = float(tap - HALF)
                masks[tap, low - first_row : low - first_row + 32, :] = jnp.where(
                    (lowest <= offset) & (highest > offset), 1.0, 0.0
                ).astype(F32)

    def prepare_taps():
        x_wide[...] = jnp.zeros_like(x_wide)
        cot_wide[...] = jnp.zeros_like(cot_wide)
        for block in range(chunks):
            place(cot_wide, block, cot_t[:, block * LANES : (block + 1) * LANES].astype(F32))
        tap_box[...] = jnp.zeros_like(tap_box)
        tap_box[0:K, 0:width] = taps[...]
        tap_box[...] = tap_box[...] + pltpu.roll(tap_box[...], 64, 1)

    def prepare_own():
        pick = (
            lax.broadcasted_iota(jnp.int32, (width, depth), 1)
            == ten * width + lax.broadcasted_iota(jnp.int32, (width, depth), 0)
        ).astype(BF16)
        own[...] = dot(pick, frames[...], 1, 1)

    edges = {}

    def rs_finish(stage, chunk, way):
        flights[stage, chunk].wait_recv()
        low, rows = starts[stage]
        if stage < 4:
            mid = rows // 2
            nxt = starts[stage + 1][0]
            rs_send[chunk, nxt : nxt + mid, :] = (
                keep[chunk, mid:rows, :] + rs_recv[chunk, low + mid : low + rows, :].astype(F32)
            ).astype(BF16)
            flights[stage + 1, chunk] = rs_start(stage + 1, chunk, way)
            keep[chunk, 0:mid, :] = keep[chunk, 0:mid, :] + rs_recv[
                chunk, low : low + mid, :
            ].astype(F32)
            return
        columns = slice(chunk * LANES, (chunk + 1) * LANES)
        branch = keep[chunk, 0:rows, :] + rs_recv[chunk, low : low + rows, :].astype(F32)
        mixed = (own[:, columns] + 0.5 * branch).astype(BF16)
        place(x_wide, chunk, mixed.astype(F32))
        if chunk == 0:
            edge_send[1] = mixed
            edges[1] = send(edge_send.at[1], edge_recv.at[1], before)
        if chunk == chunks - 1:
            edge_send[0] = mixed
            edges[0] = send(edge_send.at[0], edge_recv.at[0], after)

    for turn in range(len(units) + 5):
        if turn < len(units):
            rs_begin(turn)
        for stage in range(5):
            if 0 <= turn - 1 - stage < len(units):
                for chunk, way in units[turn - 1 - stage]:
                    rs_finish(stage, chunk, way)
        if turn == 1:
            cot_copies.append(send(cot_send.at[0], cot_recv.at[0], after))
            cot_copies.append(send(cot_send.at[1], cot_recv.at[1], before))
            prepare_taps()
        if turn == 2:
            prepare_own()
        if turn == 3:
            prepare_masks()

    for side, block in ((0, -1), (1, chunks)):
        cot_copies[side].wait_recv()
        place(cot_wide, block, cot_recv[side].astype(F32))
    turn_round(cot_wide, cot_tall)
    for side, block in ((0, -1), (1, chunks)):
        edges[side].wait_recv()
        place(x_wide, block, edge_recv[side].astype(F32))
    turn_round(x_wide, x_tall)

    spans = side_length // LANES
    step = 104
    for low in range(first_row, last_row, step):
        here = x_tall[low : low + step, :]
        conv = jnp.zeros((step, LANES), F32)
        for tap in range(K):
            moved = x_tall[low + tap - HALF : low + tap - HALF + step, :]
            mask = masks[tap, low - first_row : low - first_row + step, :]
            conv = conv + tap_box[tap : tap + 1, :] * (moved * mask)
        gate = jax.nn.sigmoid(conv)
        grad_tall[low : low + step, :] = (
            cot_tall[low : low + step, :] * gate * (1.0 + conv * (1.0 - gate))
        )
        out_tall[low : low + step, :] = here + conv * gate

    def convolve_back(unit):
        parts = []
        step = LANES // 2
        for low in range(LANES * (unit + 1), LANES * (unit + 2), step):
            here = x_tall[low : low + step, :]
            total = cot_tall[low : low + step, :]
            for tap in range(K):
                moved = grad_tall[low + HALF - tap : low + HALF - tap + step, :]
                moved = moved * masks[K - 1 - tap, low - first_row : low - first_row + step, :]
                total = total + tap_box[tap : tap + 1, :] * moved
                term = jnp.sum((moved * here).reshape(step // 8, 8, LANES), axis=0)
                if low == LANES:
                    tap_sums[tap] = term
                else:
                    tap_sums[tap] = tap_sums[tap] + term
            parts.append(total)
        return jnp.concatenate(parts, axis=0).T

    ag = {}

    def ag_start(stage, unit, way):
        first, second = WAYS[way]
        targets = (z_way(first), z_way(second), x_way(first), x_way(second), sibling, sibling)
        low, rows, move = 0, width << stage, width << stage
        if stage >= 4:
            low, rows, move = (0, half // 2, half) if stage == 4 else (half // 2, half // 2, half)
        ag[stage, unit, way] = send(
            gathered.at[unit, way, pl.ds(low, rows), :],
            gathered.at[unit, way, pl.ds(low + move, rows), :],
            targets[stage],
        )

    for unit in range(spans):
        grad_mixed = convolve_back(unit).astype(BF16)
        for way in range(2):
            gathered[unit, way, 0:width, :] = grad_mixed[64 * way : 64 * way + width, :]
            ag_start(0, unit, way)
    for unit in range(spans):
        output = out_tall[LANES * (unit + 1) : LANES * (unit + 2), :].T.astype(BF16)
        for way in range(2):
            left = side_length * way + LANES * unit
            out_t[:, left : left + LANES] = output[64 * way : 64 * way + width, :]
    tap_sums[K] = jnp.zeros((8, LANES), F32)
    sums = jnp.sum(tap_sums[...], axis=1)
    sums = sums + pltpu.roll(sums, 64, 1)
    kernel_ring[y] = sums

    taps_flight = {}

    def taps_start(hop):
        for step, hops in ((1, 4), (-1, 3)):
            if hop > hops:
                continue
            spot = lax.rem(y + NY - step * (hop - 1), NY)
            taps_flight[hop, step] = send(kernel_ring.at[spot], kernel_ring.at[spot], y_way(step))

    def taps_wait(hop):
        for step in (1, -1):
            if (hop, step) in taps_flight:
                taps_flight[hop, step].wait_recv()

    taps_start(1)

    def settle(unit, way, c):
        for i in range(NX):
            for j in range(NZ):
                home = tensor_at(
                    flip(z, relative(j, way)),
                    flip(x, relative(i, way)),
                    1 - core if c else core,
                )
                spot = (c * NX + i) * NZ + j
                piece[
                    unit,
                    pl.ds(pl.multiple_of(home * width, 16), width),
                    way * LANES : (way + 1) * LANES,
                ] = gathered[unit, way, spot * width : (spot + 1) * width, :]

    def ag_finish(stage, unit):
        for way in range(2):
            ag[stage, unit, way].wait_recv()
            if stage < 3:
                ag_start(stage + 1, unit, way)
            if stage == 2:
                ag_start(4, unit, way)
            if stage == 3:
                ag_start(5, unit, way)
        for way in range(2):
            if stage == 3:
                settle(unit, way, 0)
            if stage == 4:
                ag[5, unit, way].wait_recv()
                settle(unit, way, 1)

    tall, broad = hid // 2, depth // 4

    def of_unit(array, unit, axis):
        low = LANES * unit
        spots = (slice(low, low + LANES), slice(side_length + low, side_length + low + LANES))
        return jnp.concatenate(
            [array[:, spot] if axis else array[spot, :] for spot in spots], axis=axis
        )

    def add_chunks(stream, unit, i, product):
        for d, part in ((2 * i, product[:tall]), (2 * i + 1, product[tall:])):
            totals[stream, d] = part if unit == 0 else totals[stream, d] + part

    def down_part(unit):
        left_side = of_unit(hidden, unit, 1)
        for i in range(4):
            rows = slice(broad * i, broad * (i + 1))
            add_chunks(0, unit, i, dot(left_side, piece[unit, rows, :], 1, 1))

    def up_part(unit):
        grad_hidden = 0.5 * dot(w_down[...], piece[unit], 1, 0)
        gate = of_unit(sig, unit, 1)
        grad_act = grad_hidden * gate * (1.0 + of_unit(act, unit, 1) * (1.0 - gate))
        grad_act = grad_act.astype(BF16)
        right_side = of_unit(normed, unit, 0)
        for i in range(4):
            columns = slice(broad * i, broad * (i + 1))
            add_chunks(1, unit, i, dot(grad_act, right_side[:, columns], 1, 0))

    for turn in range(spans + 4):
        for stage in range(5):
            if 0 <= turn - stage < spans:
                ag_finish(stage, turn - stage)
        if 4 <= turn < spans + 3:
            down_part(turn - 4)
            up_part(turn - 4)
        if turn in (3, 5):
            taps_wait(turn // 2)
            taps_start(turn // 2 + 1)
    ring = {}

    def ring_spot(stream, side, k):
        return (stream * 2 + side) * 4 + k - 1

    def ring_start(stream, side, k):
        step = (1, -1)[side]
        if k > HOPS[stream][side]:
            return
        chunk = lax.rem(y + NY + step * k, NY)
        value = totals[stream, chunk]
        if k < HOPS[stream][side]:
            ring[stream, side, k + 1].wait_recv()
            value = value + ring_recv[ring_spot(stream, side, k + 1)].astype(F32)
        spot = ring_spot(stream, side, k)
        ring_send[spot] = value.astype(BF16)
        ring[stream, side, k] = send(ring_send.at[spot], ring_recv.at[spot], y_way(step))

    down_part(spans - 1)
    ring_start(0, 0, 4)
    ring_start(0, 1, 3)
    taps_wait(3)
    taps_start(4)
    up_part(spans - 1)
    ring_start(1, 1, 4)
    ring_start(1, 0, 3)
    ring_start(0, 0, 3)
    ring_start(1, 1, 3)
    taps_wait(4)
    total = kernel_ring[0]
    for i in range(1, NY):
        total = total + kernel_ring[i]
    kernel_cross[w] = total
    cross = [send(kernel_cross.at[w], kernel_cross.at[w], w_way(step)) for step in (1, 2)]
    for k in (2, 1):
        ring_start(0, 1, k)
        ring_start(1, 0, k)
        ring_start(0, 0, k)
        ring_start(1, 1, k)

    third = tall // NW
    cross_flight = {}
    for stream in range(2):
        for side in range(2):
            ring[stream, side, 1].wait_recv()
        totals[stream, y] = (
            totals[stream, y]
            + ring_recv[ring_spot(stream, 0, 1)].astype(F32)
            + ring_recv[ring_spot(stream, 1, 1)].astype(F32)
        )
        for step in (1, 2):
            rows = pl.ds(pl.multiple_of(lax.rem(w + step, NW) * third, third), third)
            cross_send[stream * 2 + step - 1] = totals[stream, y, rows, :].astype(BF16)
            cross_flight[stream, step] = send(
                cross_send.at[stream * 2 + step - 1],
                cross_recv.at[stream * 2 + step - 1],
                w_way(step),
            )
    for copy in cross:
        copy.wait_recv()
    scale = 1.0 / math.sqrt(length * count)
    summed = (kernel_cross[0] + kernel_cross[1] + kernel_cross[2]) * scale
    kernel_sum[...] = summed[0:K, 0:width]
    mine = pl.ds(pl.multiple_of(w * third, third), third)
    share = {}
    for stream in range(2):
        value = totals[stream, y, mine, :]
        for step in (1, 2):
            cross_flight[stream, step].wait_recv()
            value = value + cross_recv[stream * 2 + step - 1].astype(F32)
        whole[stream, y, mine, :] = value.astype(BF16)
        for step in (1, 2):
            share[stream, step] = send(
                whole.at[stream, y, mine, :], whole.at[stream, y, mine, :], w_way(step)
            )
    spread = {}
    for k in range(1, 6):
        for part in range(NW):
            rows = pl.ds(pl.multiple_of(lax.rem(w + NW - part, NW) * third, third), third)
            for stream in range(2):
                if k == 1 and part > 0:
                    share[stream, part].wait_recv()
                for side in range(2):
                    step = (1, -1)[side]
                    if 1 < k <= HOPS[stream][side] + 1:
                        spread[stream, side, k - 1, part].wait_recv()
                    if k <= HOPS[stream][side]:
                        spot = lax.rem(y + NY - step * (k - 1), NY)
                        spread[stream, side, k, part] = send(
                            whole.at[stream, spot, rows, :],
                            whole.at[stream, spot, rows, :],
                            y_way(step),
                        )
    grads[...] = whole[...]
    for copy in started:
        copy.wait_send()


def finish(scale, grads, out_t, kernel_sum, down, up_t, out, kernel_out):
    down[...] = grads[0].reshape(down.shape).astype(F32) * (0.5 * scale)
    up_t[...] = grads[1].reshape(up_t.shape).astype(F32) * scale
    out[...] = out_t[...]
    kernel_out[...] = kernel_sum[...]


def body(frames, w_up, w_down, taps, bounds, cot):
    length, depth = frames.shape
    width = taps.shape[1]
    hid = w_up.shape[1]
    ext = length // 2 + 2 * LANES
    chunks = length // LANES
    rs_rows = depth // 2 + depth // 4 + depth // 8 + depth // 16 + depth // 32
    block = (hid // 2, depth // 4)
    vmem = pl.BlockSpec(memory_space=pltpu.VMEM)
    out_t, kernel_sum, grads = pl.pallas_call(
        kernel,
        out_shape=(
            jax.ShapeDtypeStruct((width, length), BF16),
            jax.ShapeDtypeStruct((K, width), F32),
            jax.ShapeDtypeStruct((2, NY, *block), BF16),
        ),
        in_specs=[vmem] * 6,
        out_specs=(vmem,) * 3,
        scratch_shapes=[
            pltpu.VMEM((length, depth), BF16),
            pltpu.VMEM((depth, hid), BF16),
            pltpu.VMEM((2, depth, hid), BF16),
            pltpu.VMEM((hid, length), F32),
            pltpu.VMEM((hid, length), F32),
            pltpu.VMEM((hid, length), BF16),
            pltpu.VMEM((chunks, depth // 2, LANES), F32),
            pltpu.VMEM((chunks, rs_rows, LANES), BF16),
            pltpu.VMEM((chunks, rs_rows, LANES), BF16),
            pltpu.VMEM((width, length), F32),
            pltpu.VMEM((LANES, ext), F32),
            pltpu.VMEM((LANES, ext), F32),
            pltpu.VMEM((ext, LANES), F32),
            pltpu.VMEM((ext, LANES), F32),
            pltpu.VMEM((ext, LANES), F32),
            pltpu.VMEM((ext, LANES), F32),
            pltpu.VMEM((ext, LANES), F32),
            pltpu.VMEM((ext, LANES), F32),
            pltpu.VMEM((2, width, LANES), BF16),
            pltpu.VMEM((2, width, LANES), BF16),
            pltpu.VMEM((2, width, LANES), BF16),
            pltpu.VMEM((2, width, LANES), BF16),
            pltpu.VMEM((K, length // 2 + 32, LANES), F32),
            pltpu.VMEM((K + 1, LANES), F32),
            pltpu.VMEM((K + 1, 8, LANES), F32),
            pltpu.VMEM((chunks // 2, 2, depth, LANES), BF16),
            pltpu.VMEM((chunks // 2, depth, 2 * LANES), BF16),
            pltpu.VMEM((2, NY, *block), F32),
            pltpu.VMEM((16, *block), BF16),
            pltpu.VMEM((16, *block), BF16),
            pltpu.VMEM((4, block[0] // NW, block[1]), BF16),
            pltpu.VMEM((4, block[0] // NW, block[1]), BF16),
            pltpu.VMEM((2, NY, *block), BF16),
            pltpu.VMEM((NY, K + 1, LANES), F32),
            pltpu.VMEM((NW, K + 1, LANES), F32),
            pltpu.SemaphoreType.DMA((COPIES,)),
            pltpu.SemaphoreType.DMA((COPIES,)),
        ],
        compiler_params=pltpu.CompilerParams(
            collective_id=0, has_side_effects=True, vmem_limit_bytes=60 << 20
        ),
    )(frames, w_up.T, w_down, taps, bounds, cot.T)
    scale = 1.0 / math.sqrt(length * NY * NW)
    steps = 4
    columns = pl.BlockSpec((hid, depth // steps), lambda i: (0, i))
    out_all = pl.BlockSpec((width, length), lambda i: (0, 0))
    taps_all = pl.BlockSpec((K, width), lambda i: (0, 0))
    down, up_t, out_t, kernel_sum = pl.pallas_call(
        partial(finish, scale),
        grid=(steps,),
        out_shape=(
            jax.ShapeDtypeStruct((hid, depth), F32),
            jax.ShapeDtypeStruct((hid, depth), F32),
            jax.ShapeDtypeStruct((width, length), BF16),
            jax.ShapeDtypeStruct((K, width), F32),
        ),
        in_specs=[
            pl.BlockSpec((2, NY // steps, *block), lambda i: (0, i, 0, 0)),
            out_all,
            taps_all,
        ],
        out_specs=(columns, columns, out_all, taps_all),
    )(grads, out_t, kernel_sum)
    return out_t.T, up_t.T, down, kernel_sum


def solution(mesh):
    return jax.shard_map(
        body,
        mesh=mesh,
        in_specs=(
            P("seq", None),
            P(None, "tensor"),
            P("tensor", None),
            P(None, "tensor"),
            P(None, "seq"),
            P("seq", "tensor"),
        ),
        out_specs=(P("seq", "tensor"), P(None, "tensor"), P("tensor", None), P(None, "tensor")),
        check_vma=False,
    )
```

```python
import math
from functools import partial

import jax
import jax.numpy as jnp
from jax import lax
from jax.experimental import pallas as pl
from jax.experimental.pallas import tpu as pltpu
from jax.sharding import PartitionSpec as P

MESH = pl.DeviceIdType.MESH
K = 31
HALF = K // 2
NY, NW, NZ, NX = 8, 3, 4, 4
LANES = 128
WAYS = ((1, 3), (3, 1))
HOPS = ((4, 3), (3, 4))
COPIES = 143
F32, BF16 = jnp.float32, jnp.bfloat16


def flip(index, mask):
    if mask == 0:
        return index
    if mask == 1:
        return index + 1 - 2 * lax.rem(index, 2)
    if mask == 2:
        return lax.rem(index + 2, 4)
    return 3 - index


def relative(place, way):
    first, second = WAYS[way]
    return (first if place & 1 else 0) ^ (second if place & 2 else 0)


def dot(a, b, a_dim, b_dim):
    return lax.dot_general(a, b, (((a_dim,), (b_dim,)), ((), ())), preferred_element_type=F32)


def kernel(
    frames,
    w_up_t,
    w_down,
    taps,
    bounds,
    cot_t,
    out_t,
    kernel_sum,
    grads,
    normed,
    w_down_t,
    ordered,
    act,
    sig,
    hidden,
    keep,
    rs_send,
    rs_recv,
    own,
    x_wide,
    cot_wide,
    x_tall,
    cot_tall,
    grad_tall,
    out_tall,
    first_tall,
    last_tall,
    edge_send,
    edge_recv,
    cot_send,
    cot_recv,
    masks,
    tap_box,
    tap_sums,
    gathered,
    piece,
    totals,
    ring_send,
    ring_recv,
    cross_send,
    cross_recv,
    whole,
    kernel_ring,
    kernel_cross,
    send_sems,
    recv_sems,
):
    length, depth = frames.shape
    width = taps.shape[1]
    hid = w_up_t.shape[0]
    side_length = length // 2
    ext = side_length + 2 * LANES
    seq, ten = lax.axis_index("seq"), lax.axis_index("tensor")
    y, w = lax.div(seq, NW), lax.rem(seq, NW)
    core, x, z = lax.rem(ten, 2), lax.rem(lax.div(ten, 2), NX), lax.div(ten, 2 * NX)

    def tensor_at(z, x, core):
        return (z * NX + x) * 2 + core

    def x_way(mask):
        return (seq, tensor_at(z, flip(x, mask), core))

    def z_way(mask):
        return (seq, tensor_at(flip(z, mask), x, core))

    def y_way(step):
        return (lax.rem(y + NY + step, NY) * NW + w, ten)

    def w_way(step):
        return (y * NW + lax.rem(w + step, NW), ten)

    sibling = (seq, tensor_at(z, x, 1 - core))
    count = NY * NW
    after = (lax.rem(seq + 1, count), ten)
    before = (lax.rem(seq + count - 1, count), ten)

    barrier = pltpu.get_barrier_semaphore()
    partners = [sibling, x_way(1), x_way(3), z_way(1), z_way(3), after, before]
    partners += [y_way(1), y_way(-1), w_way(1), w_way(2)]
    for partner in partners:
        pl.semaphore_signal(barrier, inc=1, device_id=partner, device_id_type=MESH)

    started = []

    def send(src, dst, target):
        spot = len(started)
        copy = pltpu.make_async_remote_copy(
            src_ref=src,
            dst_ref=dst,
            send_sem=send_sems.at[spot],
            recv_sem=recv_sems.at[spot],
            device_id=target,
            device_id_type=MESH,
        )
        copy.start()
        started.append(copy)
        return copy

    w_down_t[...] = w_down[...].astype(F32).T.astype(BF16)
    for way in range(2):
        for c in range(2):
            for i in range(NX):
                for j in range(NZ):
                    home = tensor_at(
                        flip(z, relative(j, way)),
                        flip(x, relative(i, way)),
                        1 - core if c else core,
                    )
                    spot = (c * NX + i) * NZ + j
                    ordered[way, spot * width : (spot + 1) * width, :] = w_down_t[
                        pl.ds(pl.multiple_of(home * width, 16), width), :
                    ]
    cot_send[0] = cot_t[:, length - LANES :]
    cot_send[1] = cot_t[:, :LANES]

    half = depth // 2
    starts, height = [], half
    offset = 0
    for _ in range(5):
        starts.append((offset, height))
        offset += height
        height //= 2
    chunks = length // LANES
    units = [((i, 0), (chunks - 1 - i, 1)) for i in range(chunks // 2)]

    def rs_start(stage, chunk, way):
        first, second = WAYS[way]
        target = (sibling, x_way(second), x_way(first), z_way(second), z_way(first))[stage]
        low, rows = starts[stage]
        return send(
            rs_send.at[chunk, pl.ds(low, rows), :], rs_recv.at[chunk, pl.ds(low, rows), :], target
        )

    flights = {}
    cot_copies = []
    first_row, last_row = LANES - 16, LANES + side_length + 16

    def place(wide, block, value):
        if block <= ext // LANES - 2:
            wide[0:width, (block + 1) * LANES : (block + 2) * LANES] = value
        shifted = block - side_length // LANES
        if shifted >= -1:
            wide[64 : 64 + width, (shifted + 1) * LANES : (shifted + 2) * LANES] = value

    def turn_round(wide, tall):
        for low in range(0, ext, LANES):
            tall[low : low + LANES, :] = wide[:, low : low + LANES].T

    def hidden_chunk(chunk):
        rows = slice(chunk * LANES, (chunk + 1) * LANES)
        wide = frames[rows, :].astype(F32)
        mean = jnp.mean(wide, axis=1, keepdims=True)
        centred = wide - mean
        var = jnp.mean(centred * centred, axis=1, keepdims=True)
        normed[rows, :] = (centred / jnp.sqrt(var + 1e-05)).astype(BF16)
        up = dot(w_up_t[...], normed[rows, :], 1, 1)
        gate = jax.nn.sigmoid(up)
        act[:, rows] = up
        sig[:, rows] = gate
        hidden[:, rows] = (up * gate).astype(BF16)

    def rs_begin(turn):
        unit = units[turn]
        for chunk, _ in unit:
            hidden_chunk(chunk)
        if turn == 0:
            pl.semaphore_wait(barrier, len(partners))
        for chunk, way in unit:
            part = hidden[:, chunk * LANES : (chunk + 1) * LANES]
            rs_send[chunk, 0:half, :] = dot(ordered[way, half:, :], part, 1, 0).astype(BF16)
            flights[0, chunk] = rs_start(0, chunk, way)
        for chunk, way in unit:
            part = hidden[:, chunk * LANES : (chunk + 1) * LANES]
            keep[chunk] = dot(ordered[way, :half, :], part, 1, 0)

    def prepare_masks():
        limits = bounds[...]
        limits = jnp.concatenate(
            [
                jnp.broadcast_to(limits[:, :1], (2, LANES)),
                limits,
                jnp.broadcast_to(limits[:, length - 1 :], (2, LANES)),
            ],
            axis=1,
        )
        spots = seq * length - LANES + lax.broadcasted_iota(jnp.int32, limits.shape, 1)
        limits = (limits - spots).astype(F32)
        for row, tall in ((0, first_tall), (1, last_tall)):
            for low in range(0, ext, LANES):
                tall[low : low + LANES, :] = jnp.concatenate(
                    [
                        jnp.broadcast_to(limits[row : row + 1, low + i : low + i + LANES], (64, LANES))
                        for i in (0, side_length)
                    ],
                    axis=0,
                ).T
        for low in range(first_row, last_row, 32):
            lowest, highest = first_tall[low : low + 32, :], last_tall[low : low + 32, :]
            for tap in range(K):
                offset = float(tap - HALF)
                masks[tap, low - first_row : low - first_row + 32, :] = jnp.where(
                    (lowest <= offset) & (highest > offset), 1.0, 0.0
                ).astype(F32)

    def prepare_taps():
        x_wide[...] = jnp.zeros_like(x_wide)
        cot_wide[...] = jnp.zeros_like(cot_wide)
        for block in range(chunks):
            place(cot_wide, block, cot_t[:, block * LANES : (block + 1) * LANES].astype(F32))
        tap_box[...] = jnp.zeros_like(tap_box)
        tap_box[0:K, 0:width] = taps[...]
        tap_box[...] = tap_box[...] + pltpu.roll(tap_box[...], 64, 1)

    def prepare_own():
        pick = (
            lax.broadcasted_iota(jnp.int32, (width, depth), 1)
            == ten * width + lax.broadcasted_iota(jnp.int32, (width, depth), 0)
        ).astype(BF16)
        own[...] = dot(pick, frames[...], 1, 1)

    edges = {}

    def rs_finish(stage, chunk, way):
        flights[stage, chunk].wait_recv()
        low, rows = starts[stage]
        if stage < 4:
            mid = rows // 2
            nxt = starts[stage + 1][0]
            rs_send[chunk, nxt : nxt + mid, :] = (
                keep[chunk, mid:rows, :] + rs_recv[chunk, low + mid : low + rows, :].astype(F32)
            ).astype(BF16)
            flights[stage + 1, chunk] = rs_start(stage + 1, chunk, way)
            keep[chunk, 0:mid, :] = keep[chunk, 0:mid, :] + rs_recv[
                chunk, low : low + mid, :
            ].astype(F32)
            return
        columns = slice(chunk * LANES, (chunk + 1) * LANES)
        branch = keep[chunk, 0:rows, :] + rs_recv[chunk, low : low + rows, :].astype(F32)
        mixed = (own[:, columns] + 0.5 * branch).astype(BF16)
        place(x_wide, chunk, mixed.astype(F32))
        if chunk == 0:
            edge_send[1] = mixed
            edges[1] = send(edge_send.at[1], edge_recv.at[1], before)
        if chunk == chunks - 1:
            edge_send[0] = mixed
            edges[0] = send(edge_send.at[0], edge_recv.at[0], after)

    for turn in range(len(units) + 5):
        if turn < len(units):
            rs_begin(turn)
        for stage in range(5):
            if 0 <= turn - 1 - stage < len(units):
                for chunk, way in units[turn - 1 - stage]:
                    rs_finish(stage, chunk, way)
        if turn == 1:
            cot_copies.append(send(cot_send.at[0], cot_recv.at[0], after))
            cot_copies.append(send(cot_send.at[1], cot_recv.at[1], before))
            prepare_taps()
        if turn == 2:
            prepare_own()
        if turn == 3:
            prepare_masks()

    for side, block in ((0, -1), (1, chunks)):
        cot_copies[side].wait_recv()
        place(cot_wide, block, cot_recv[side].astype(F32))
    turn_round(cot_wide, cot_tall)
    for side, block in ((0, -1), (1, chunks)):
        edges[side].wait_recv()
        place(x_wide, block, edge_recv[side].astype(F32))
    turn_round(x_wide, x_tall)

    spans = side_length // LANES
    step = 104

    def convolve(block):
        low = first_row + step * block
        here = x_tall[low : low + step, :]
        conv = jnp.zeros((step, LANES), F32)
        for tap in range(K):
            moved = x_tall[low + tap - HALF : low + tap - HALF + step, :]
            mask = masks[tap, low - first_row : low - first_row + step, :]
            conv = conv + tap_box[tap : tap + 1, :] * (moved * mask)
        gate = jax.nn.sigmoid(conv)
        grad_tall[low : low + step, :] = (
            cot_tall[low : low + step, :] * gate * (1.0 + conv * (1.0 - gate))
        )
        out_tall[low : low + step, :] = here + conv * gate

    def convolve_back(unit):
        parts = []
        step = LANES // 2
        for low in range(LANES * (unit + 1), LANES * (unit + 2), step):
            here = x_tall[low : low + step, :]
            total = cot_tall[low : low + step, :]
            for tap in range(K):
                moved = grad_tall[low + HALF - tap : low + HALF - tap + step, :]
                moved = moved * masks[K - 1 - tap, low - first_row : low - first_row + step, :]
                total = total + tap_box[tap : tap + 1, :] * moved
                term = jnp.sum((moved * here).reshape(step // 8, 8, LANES), axis=0)
                if low == LANES:
                    tap_sums[tap] = term
                else:
                    tap_sums[tap] = tap_sums[tap] + term
            parts.append(total)
        return jnp.concatenate(parts, axis=0).T

    ag = {}

    def ag_start(stage, unit, way):
        first, second = WAYS[way]
        targets = (z_way(first), z_way(second), x_way(first), x_way(second), sibling, sibling)
        low, rows, move = 0, width << stage, width << stage
        if stage >= 4:
            low, rows, move = (0, half // 2, half) if stage == 4 else (half // 2, half // 2, half)
        ag[stage, unit, way] = send(
            gathered.at[unit, way, pl.ds(low, rows), :],
            gathered.at[unit, way, pl.ds(low + move, rows), :],
            targets[stage],
        )

    convolve(0)
    for unit in range(spans):
        convolve(unit + 1)
        grad_mixed = convolve_back(unit).astype(BF16)
        for way in range(2):
            gathered[unit, way, 0:width, :] = grad_mixed[64 * way : 64 * way + width, :]
            ag_start(0, unit, way)
    for unit in range(spans):
        output = out_tall[LANES * (unit + 1) : LANES * (unit + 2), :].T.astype(BF16)
        for way in range(2):
            left = side_length * way + LANES * unit
            out_t[:, left : left + LANES] = output[64 * way : 64 * way + width, :]
    tap_sums[K] = jnp.zeros((8, LANES), F32)
    sums = jnp.sum(tap_sums[...], axis=1)
    sums = sums + pltpu.roll(sums, 64, 1)
    kernel_ring[y] = sums

    taps_flight = {}

    def taps_start(hop):
        for step, hops in ((1, 4), (-1, 3)):
            if hop > hops:
                continue
            spot = lax.rem(y + NY - step * (hop - 1), NY)
            taps_flight[hop, step] = send(kernel_ring.at[spot], kernel_ring.at[spot], y_way(step))

    def taps_wait(hop):
        for step in (1, -1):
            if (hop, step) in taps_flight:
                taps_flight[hop, step].wait_recv()

    taps_start(1)

    def settle(unit, way, c):
        for i in range(NX):
            for j in range(NZ):
                home = tensor_at(
                    flip(z, relative(j, way)),
                    flip(x, relative(i, way)),
                    1 - core if c else core,
                )
                spot = (c * NX + i) * NZ + j
                piece[
                    unit,
                    pl.ds(pl.multiple_of(home * width, 16), width),
                    way * LANES : (way + 1) * LANES,
                ] = gathered[unit, way, spot * width : (spot + 1) * width, :]

    def ag_finish(stage, unit):
        for way in range(2):
            ag[stage, unit, way].wait_recv()
            if stage < 3:
                ag_start(stage + 1, unit, way)
            if stage == 2:
                ag_start(4, unit, way)
            if stage == 3:
                ag_start(5, unit, way)
        for way in range(2):
            if stage == 3:
                settle(unit, way, 0)
            if stage == 4:
                ag[5, unit, way].wait_recv()
                settle(unit, way, 1)

    tall, broad = hid // 2, depth // 4

    def of_unit(array, unit, axis):
        low = LANES * unit
        spots = (slice(low, low + LANES), slice(side_length + low, side_length + low + LANES))
        return jnp.concatenate(
            [array[:, spot] if axis else array[spot, :] for spot in spots], axis=axis
        )

    def add_chunks(stream, unit, i, product):
        for d, part in ((2 * i, product[:tall]), (2 * i + 1, product[tall:])):
            totals[stream, d] = part if unit == 0 else totals[stream, d] + part

    def down_part(unit):
        left_side = of_unit(hidden, unit, 1)
        for i in range(4):
            rows = slice(broad * i, broad * (i + 1))
            add_chunks(0, unit, i, dot(left_side, piece[unit, rows, :], 1, 1))

    def up_part(unit):
        grad_hidden = 0.5 * dot(w_down[...], piece[unit], 1, 0)
        gate = of_unit(sig, unit, 1)
        grad_act = grad_hidden * gate * (1.0 + of_unit(act, unit, 1) * (1.0 - gate))
        grad_act = grad_act.astype(BF16)
        right_side = of_unit(normed, unit, 0)
        for i in range(4):
            columns = slice(broad * i, broad * (i + 1))
            add_chunks(1, unit, i, dot(grad_act, right_side[:, columns], 1, 0))

    for turn in range(spans + 4):
        for stage in range(5):
            if 0 <= turn - stage < spans:
                ag_finish(stage, turn - stage)
        if 4 <= turn < spans + 3:
            down_part(turn - 4)
            up_part(turn - 4)
        if turn in (3, 5):
            taps_wait(turn // 2)
            taps_start(turn // 2 + 1)
    ring = {}

    def ring_spot(stream, side, k):
        return (stream * 2 + side) * 4 + k - 1

    def ring_start(stream, side, k):
        step = (1, -1)[side]
        if k > HOPS[stream][side]:
            return
        chunk = lax.rem(y + NY + step * k, NY)
        value = totals[stream, chunk]
        if k < HOPS[stream][side]:
            ring[stream, side, k + 1].wait_recv()
            value = value + ring_recv[ring_spot(stream, side, k + 1)].astype(F32)
        spot = ring_spot(stream, side, k)
        ring_send[spot] = value.astype(BF16)
        ring[stream, side, k] = send(ring_send.at[spot], ring_recv.at[spot], y_way(step))

    down_part(spans - 1)
    ring_start(0, 0, 4)
    ring_start(0, 1, 3)
    taps_wait(3)
    taps_start(4)
    up_part(spans - 1)
    ring_start(1, 1, 4)
    ring_start(1, 0, 3)
    ring_start(0, 0, 3)
    ring_start(1, 1, 3)
    taps_wait(4)
    total = kernel_ring[0]
    for i in range(1, NY):
        total = total + kernel_ring[i]
    kernel_cross[w] = total
    cross = [send(kernel_cross.at[w], kernel_cross.at[w], w_way(step)) for step in (1, 2)]
    for k in (2, 1):
        ring_start(0, 1, k)
        ring_start(1, 0, k)
        ring_start(0, 0, k)
        ring_start(1, 1, k)

    third = tall // NW
    cross_flight = {}
    for stream in range(2):
        for side in range(2):
            ring[stream, side, 1].wait_recv()
        totals[stream, y] = (
            totals[stream, y]
            + ring_recv[ring_spot(stream, 0, 1)].astype(F32)
            + ring_recv[ring_spot(stream, 1, 1)].astype(F32)
        )
        for step in (1, 2):
            rows = pl.ds(pl.multiple_of(lax.rem(w + step, NW) * third, third), third)
            cross_send[stream * 2 + step - 1] = totals[stream, y, rows, :].astype(BF16)
            cross_flight[stream, step] = send(
                cross_send.at[stream * 2 + step - 1],
                cross_recv.at[stream * 2 + step - 1],
                w_way(step),
            )
    for copy in cross:
        copy.wait_recv()
    scale = 1.0 / math.sqrt(length * count)
    summed = (kernel_cross[0] + kernel_cross[1] + kernel_cross[2]) * scale
    kernel_sum[...] = summed[0:K, 0:width]
    mine = pl.ds(pl.multiple_of(w * third, third), third)
    share = {}
    for stream in range(2):
        value = totals[stream, y, mine, :]
        for step in (1, 2):
            cross_flight[stream, step].wait_recv()
            value = value + cross_recv[stream * 2 + step - 1].astype(F32)
        whole[stream, y, mine, :] = value.astype(BF16)
        for step in (1, 2):
            share[stream, step] = send(
                whole.at[stream, y, mine, :], whole.at[stream, y, mine, :], w_way(step)
            )
    spread = {}
    for k in range(1, 6):
        for part in range(NW):
            rows = pl.ds(pl.multiple_of(lax.rem(w + NW - part, NW) * third, third), third)
            for stream in range(2):
                if k == 1 and part > 0:
                    share[stream, part].wait_recv()
                for side in range(2):
                    step = (1, -1)[side]
                    if 1 < k <= HOPS[stream][side] + 1:
                        spread[stream, side, k - 1, part].wait_recv()
                    if k <= HOPS[stream][side]:
                        spot = lax.rem(y + NY - step * (k - 1), NY)
                        spread[stream, side, k, part] = send(
                            whole.at[stream, spot, rows, :],
                            whole.at[stream, spot, rows, :],
                            y_way(step),
                        )
    grads[...] = whole[...]
    for copy in started:
        copy.wait_send()


def finish(scale, grads, out_t, kernel_sum, down, up_t, out, kernel_out):
    hid, broad = down.shape[0], grads.shape[3]
    for i in range(NY // 2):
        columns = slice(broad * i, broad * (i + 1))
        pair = slice(2 * i, 2 * i + 2)
        down[:, columns] = grads[0, pair].reshape(hid, broad).astype(F32) * (0.5 * scale)
        up_t[:, columns] = grads[1, pair].reshape(hid, broad).astype(F32) * scale
    out[...] = out_t[...]
    kernel_out[...] = kernel_sum[...]


def body(frames, w_up, w_down, taps, bounds, cot):
    length, depth = frames.shape
    width = taps.shape[1]
    hid = w_up.shape[1]
    ext = length // 2 + 2 * LANES
    chunks = length // LANES
    rs_rows = depth // 2 + depth // 4 + depth // 8 + depth // 16 + depth // 32
    block = (hid // 2, depth // 4)
    vmem = pl.BlockSpec(memory_space=pltpu.VMEM)
    out_t, kernel_sum, grads = pl.pallas_call(
        kernel,
        out_shape=(
            jax.ShapeDtypeStruct((width, length), BF16),
            jax.ShapeDtypeStruct((K, width), F32),
            jax.ShapeDtypeStruct((2, NY, *block), BF16),
        ),
        in_specs=[vmem] * 6,
        out_specs=(vmem,) * 3,
        scratch_shapes=[
            pltpu.VMEM((length, depth), BF16),
            pltpu.VMEM((depth, hid), BF16),
            pltpu.VMEM((2, depth, hid), BF16),
            pltpu.VMEM((hid, length), F32),
            pltpu.VMEM((hid, length), F32),
            pltpu.VMEM((hid, length), BF16),
            pltpu.VMEM((chunks, depth // 2, LANES), F32),
            pltpu.VMEM((chunks, rs_rows, LANES), BF16),
            pltpu.VMEM((chunks, rs_rows, LANES), BF16),
            pltpu.VMEM((width, length), F32),
            pltpu.VMEM((LANES, ext), F32),
            pltpu.VMEM((LANES, ext), F32),
            pltpu.VMEM((ext, LANES), F32),
            pltpu.VMEM((ext, LANES), F32),
            pltpu.VMEM((ext, LANES), F32),
            pltpu.VMEM((ext, LANES), F32),
            pltpu.VMEM((ext, LANES), F32),
            pltpu.VMEM((ext, LANES), F32),
            pltpu.VMEM((2, width, LANES), BF16),
            pltpu.VMEM((2, width, LANES), BF16),
            pltpu.VMEM((2, width, LANES), BF16),
            pltpu.VMEM((2, width, LANES), BF16),
            pltpu.VMEM((K, length // 2 + 32, LANES), F32),
            pltpu.VMEM((K + 1, LANES), F32),
            pltpu.VMEM((K + 1, 8, LANES), F32),
            pltpu.VMEM((chunks // 2, 2, depth, LANES), BF16),
            pltpu.VMEM((chunks // 2, depth, 2 * LANES), BF16),
            pltpu.VMEM((2, NY, *block), F32),
            pltpu.VMEM((16, *block), BF16),
            pltpu.VMEM((16, *block), BF16),
            pltpu.VMEM((4, block[0] // NW, block[1]), BF16),
            pltpu.VMEM((4, block[0] // NW, block[1]), BF16),
            pltpu.VMEM((2, NY, *block), BF16),
            pltpu.VMEM((NY, K + 1, LANES), F32),
            pltpu.VMEM((NW, K + 1, LANES), F32),
            pltpu.SemaphoreType.DMA((COPIES,)),
            pltpu.SemaphoreType.DMA((COPIES,)),
        ],
        compiler_params=pltpu.CompilerParams(
            collective_id=0, has_side_effects=True, vmem_limit_bytes=60 << 20
        ),
    )(frames, w_up.T, w_down, taps, bounds, cot.T)
    scale = 1.0 / math.sqrt(length * NY * NW)
    down, up_t, out_t, kernel_sum = pl.pallas_call(
        partial(finish, scale),
        out_shape=(
            jax.ShapeDtypeStruct((hid, depth), F32),
            jax.ShapeDtypeStruct((hid, depth), F32),
            jax.ShapeDtypeStruct((width, length), BF16),
            jax.ShapeDtypeStruct((K, width), F32),
        ),
        in_specs=[vmem] * 3,
        out_specs=(vmem,) * 4,
    )(grads, out_t, kernel_sum)
    return out_t.T, up_t.T, down, kernel_sum


def solution(mesh):
    return jax.shard_map(
        body,
        mesh=mesh,
        in_specs=(
            P("seq", None),
            P(None, "tensor"),
            P("tensor", None),
            P(None, "tensor"),
            P(None, "seq"),
            P("seq", "tensor"),
        ),
        out_specs=(P("seq", "tensor"), P(None, "tensor"), P("tensor", None), P(None, "tensor")),
        check_vma=False,
    )
```
